128 devices in a mesh: member: 4 (over y), tile: 32 (over x, z, core).
Axes of the slice: x: 4, y: 4, z: 4, core: 2. Of those that a mesh axis runs over, the one named last changes fastest.
Arguments:
- alpha: float32 [80, 4, 64, 1440], P('member', None, 'tile'), may hold values from -6 to 6
- ensemble: bfloat16 [80, 4, 4, 64, 1440], P('member', None, None, 'tile'), may hold values from -6 to 6
- step_count: int32 [4], replicated, may hold values from 1 to 8
- obs_index: int32 [32, 32, 4, 1024], P('tile'), may hold values from 0 to 46079, as said below
- obs_weight: float32 [32, 32, 4, 1024], P('tile'), may hold values from 0 to 0.5
- obs_count: int32 [32, 32], P('tile'), may hold values from 0 to 1024
- obs_value: float32 [32, 32, 1024], P(None, 'tile'), may hold values from -6 to 6
- inv_var: float32 [32, 32, 1024], P(None, 'tile'), may hold values from 2 to 32
Outputs:
- gradient: float32 [80, 4, 64, 1440], P('member', None, 'tile')
- departure: float32 [32, 32, 1024], P('tile')
The draws below stay inside these ranges and needn't reach their ends.
Inputs may be any that keep to these rules, and one draw needn't show every extreme that they name: `obs_index`: all four corners of a slot name one field and level; they are two neighbouring rows of the owner tile and two neighbouring columns, the column after the last being the first.
All inputs are finite; a program needn't handle non-finite values.
Results may differ from the reference program's by a relative error of at most 0.0003.
Values sent between devices are 32-bit elements; how exact they have to be, the bound alone decides.
No kernel may reach another device: no remote copies, remote signals or barrier semaphores. Data moves between devices by JAX's collectives and lax.ppermute only.
A program may use at most 64 MiB of HBM per device.

```python
import math
import jax
import jax.numpy as jnp
from jax import lax

FLD = 4
LON = 1440
LEV = 4
ROWS_DEV = 2
SLOT = 1024
KMAX = 8
MEMBERS = 80
LAT = 64
N_TILE = 32


def draw_step_count(key, part):
    key = jax.random.fold_in(key, 11)
    first, second = jax.random.split(key)
    counts = jax.random.randint(first, (LEV,), 1, KMAX + 1)
    where_top = jax.random.randint(second, (), 0, LEV)
    levels = jnp.arange(LEV, dtype=jnp.int32)
    counts = jnp.where(levels == where_top, KMAX, counts)
    counts = jnp.where(levels == (where_top + 1) % LEV, 1, counts)
    return counts.astype(jnp.int32)


def draw_obs_count(key, part):
    key = jax.random.fold_in(key, 12)
    first, second = jax.random.split(key)
    counts = jax.random.randint(first, (N_TILE, N_TILE), 0, SLOT + 1)
    column = jax.random.randint(second, (N_TILE,), 0, N_TILE)
    tiles = jnp.arange(N_TILE, dtype=jnp.int32)
    counts = jnp.where(tiles[None, :] == column[:, None], SLOT, counts)
    return counts.astype(jnp.int32)


def draw_obs_index(key, part):
    key = jax.random.fold_in(key, 13)
    first, second, third = jax.random.split(key, 3)
    shape = (N_TILE, N_TILE, 1, SLOT)
    channel = jax.random.randint(first, shape, 0, FLD * LEV)
    row = jax.random.randint(second, shape, 0, ROWS_DEV - 1)
    column = jax.random.randint(third, shape, 0, LON)
    channel = channel.at[0, 0, 0, 0].set(FLD * LEV - 1).at[0, 0, 0, 1].set(0)
    row = row.at[0, 0, 0, 0].set(ROWS_DEV - 2).at[0, 0, 0, 1].set(0)
    column = column.at[0, 0, 0, 0].set(LON - 1).at[0, 0, 0, 1].set(0)
    right = (column + 1) % LON
    rows_all = jnp.concatenate([row, row, row + 1, row + 1], axis=2)
    cols_all = jnp.concatenate([column, right, column, right], axis=2)
    chans = jnp.concatenate([channel, channel, channel, channel], axis=2)
    return (chans * (ROWS_DEV * LON) + rows_all * LON + cols_all).astype(jnp.int32)


def block_scale(key, shape, cuts, smallest, high):
    level = 1.0
    for axis_at, parts in cuts:
        steps = jax.random.uniform(jax.random.fold_in(jax.random.fold_in(key, 6), axis_at), (parts,), jnp.float32, smallest / len(cuts), high / len(cuts))
        level = level * jnp.repeat(jnp.exp(steps), shape[axis_at] // parts).reshape((-1,) + (1,) * (len(shape) - 1 - axis_at))
    return level


def normal_values(key, shape, deviation, limit, shards=(), kind=jnp.bfloat16):
    values = deviation * jax.random.normal(key, shape, jnp.float32)
    if shards:
        values = values * block_scale(key, shape, shards, -0.22, 0.18)
    return jnp.clip(values, -limit, limit).astype(kind)


def setup_inputs(seed: int = 0) -> dict:
    key_list = jax.random.split(jax.random.key(seed), 9)
    alpha = normal_values(key_list[0], (MEMBERS, LEV, LAT, LON), 1.0, 6.0, ((0, 4), (2, 32)), jnp.float32)
    ensemble = normal_values(key_list[1], (MEMBERS, FLD, LEV, LAT, LON), 1.0, 6.0, ((0, 4), (3, 32)))
    step_count = draw_step_count(jax.random.fold_in(key_list[8], 71), 0)
    obs_index = draw_obs_index(jax.random.fold_in(key_list[8], 71), 0)
    obs_weight = jnp.clip(0.5 * jax.random.uniform(key_list[4], (N_TILE, N_TILE, 4, SLOT), jnp.float32) ** block_scale(key_list[4], (N_TILE, N_TILE, 4, SLOT), ((0, 32),), -0.2, 0.2), 0.0, 0.5)
    obs_count = draw_obs_count(jax.random.fold_in(key_list[8], 71), 0)
    obs_value = normal_values(key_list[6], (N_TILE, N_TILE, SLOT), 1.0, 6.0, ((1, 32),), jnp.float32)
    inv_var = jnp.clip(jnp.exp(math.log(32.0) - 2.7725887 * jax.random.uniform(key_list[7], (N_TILE, N_TILE, SLOT), jnp.float32) ** block_scale(key_list[7], (N_TILE, N_TILE, SLOT), ((1, 32),), -0.2, 0.2)), 2.0, 32.0)
    return {"alpha": alpha, "ensemble": ensemble, "step_count": step_count, "obs_index": obs_index, "obs_weight": obs_weight, "obs_count": obs_count, "obs_value": obs_value, "inv_var": inv_var}


def diffuse(field, step_count):
    value = field
    for step in range(KMAX):
        active = (step < step_count).astype(jnp.float32)
        padded = jnp.pad(value, ((0, 0), (1, 1), (0, 0)))
        laplace = padded[:, :-2] + padded[:, 2:] + jnp.roll(value, 1, 2) + jnp.roll(value, -1, 2) - 4.0 * value
        value = value + 0.2 * active[:, None, None] * laplace
    return value

def reference(alpha, ensemble, step_count, obs_index, obs_weight, obs_count, obs_value, inv_var):
    scale = 1.0 / math.sqrt(MEMBERS - 1)

    def add_member(total, pair):
        member_alpha, member_ens = pair
        local = diffuse(member_alpha, step_count)
        return (total + member_ens.astype(jnp.float32) * local[None], None)
    start = jnp.zeros((FLD, LEV, LAT, LON), jnp.float32)
    summed, unused = lax.scan(add_member, start, (alpha, ensemble))
    increment = summed * scale
    blocks = increment.reshape(FLD, LEV, N_TILE, ROWS_DEV, LON).transpose(2, 0, 1, 3, 4).reshape(N_TILE, -1)
    picked = jax.vmap(lambda block, index: block[index])(blocks, obs_index)
    model_obs = lax.optimization_barrier(jnp.sum(obs_weight * picked, axis=2))
    weighted = inv_var * (obs_value - model_obs)
    live = jnp.arange(SLOT, dtype=jnp.int32)[None, None, :] < obs_count[:, :, None]
    departure = jnp.where(live, weighted, jnp.float32(0.0))
    spread = obs_weight * departure[:, :, None, :]
    size_block = FLD * LEV * ROWS_DEV * LON
    adjoint_blocks = jax.vmap(lambda index, term: jax.ops.segment_sum(term.ravel(), index.ravel(), size_block))(obs_index, spread)
    adjoint = adjoint_blocks.reshape(N_TILE, FLD, LEV, ROWS_DEV, LON).transpose(1, 2, 0, 3, 4).reshape(FLD, LEV, LAT, LON)

    def member_gradient(pair):
        member_alpha, member_ens = pair
        project = lax.optimization_barrier(jnp.sum(member_ens.astype(jnp.float32) * adjoint, axis=0)) * scale
        return member_alpha - diffuse(project, step_count)
    gradient = lax.map(member_gradient, (alpha, ensemble))
    return (gradient, departure)
```

```python
import math

import jax
import jax.numpy as jnp
from jax import lax
from jax.experimental import pallas as pl
from jax.experimental.pallas import tpu as pltpu
from jax.sharding import PartitionSpec as P

FLD, LEV, ROWS, LON = 4, 4, 2, 1440
TILES, SLOT, GROUP = 32, 1024, 20
LAT = TILES * ROWS
CH = FLD * LEV
KMAX = 8

PIECES = 5
MGRP = GROUP // PIECES
HALF = LON // 2
PIECE = HALF + 2 * KMAX
LANES = 128
LINE = -(-PIECES * PIECE // LANES)
COLS = -(-LON // LANES)
OBS_ROWS = SLOT // LANES
LINE_OBS = LINE + OBS_ROWS

CHUNK = 90
CHUNKS = LON // CHUNK
HI = CH * CHUNKS
LO = 96
BLOCK = 256
PER_SRC = SLOT // BLOCK
BLOCKS = TILES * PER_SRC

F32, BF16, I32 = jnp.float32, jnp.bfloat16, jnp.int32
VMEM = pl.BlockSpec(memory_space=pltpu.VMEM)
SMEM = pl.BlockSpec(memory_space=pltpu.SMEM)


def params(mib):
    return pltpu.CompilerParams(vmem_limit_bytes=mib * 1024 * 1024)


def lanes8():
    return lax.broadcasted_iota(I32, (8, LANES), 1)


def assemble(fetch, where_from, cache):
    value, start, last = None, 0, None
    segments = []
    for lane in range(LANES):
        src = where_from(lane)
        if src is None:
            continue
        key, tile, at = src
        this = (key, tile, (lane - at) % LANES)
        if this != last:
            segments.append((lane, this))
            last = this
    for start, (key, tile, shift) in segments:
        if (key, tile, shift) not in cache:
            x = fetch(key, tile)
            cache[key, tile, shift] = pltpu.roll(x, shift, 1) if shift else x
        x = cache[key, tile, shift]
        value = x if value is None else jnp.where(lanes8() >= start, x, value)
    return value


def pack_rows(fetch, store, line):
    for mgrp in range(MGRP):
        for half in range(2):
            cache = {}
            for j in range(LINE):

                def where_from(lane):
                    piece, at = divmod(j * LANES + lane, PIECE)
                    if piece >= PIECES:
                        return None
                    col = (at - KMAX + half * HALF) % LON
                    return (piece, col // LANES, col % LANES)

                tile = assemble(lambda piece, t: fetch(piece * MGRP + mgrp, t), where_from, cache)
                store((half * MGRP * 8 + mgrp * 8) * line + j, tile)


def unpack_tile(got_ref, member, t, cache):
    piece, mgrp = divmod(member, MGRP)

    def where_from(lane):
        col = t * LANES + lane
        if col >= LON:
            return None
        half, at = divmod(col, HALF)
        at += piece * PIECE + KMAX
        return (half, at // LANES, at % LANES)

    def fetch(half, j):
        return got_ref[pl.ds((half * MGRP * 8 + mgrp * 8) * LINE + j, 8, stride=LINE), :]

    return assemble(fetch, where_from, cache)


def pack_kernel(alpha_ref, value_ref, var_ref, out_ref):
    def fetch(member, t):
        return alpha_ref[member * 8 : member * 8 + 8, t * LANES : (t + 1) * LANES]

    def store(row, tile):
        out_ref[pl.ds(row, 8, stride=LINE_OBS), :] = tile

    pack_rows(fetch, store, LINE_OBS)
    for d in range(TILES):
        for r, ref in enumerate((value_ref, var_ref)):
            at = (d * 2 + r) * LINE_OBS + LINE
            out_ref[at : at + OBS_ROWS, :] = ref[d * OBS_ROWS : (d + 1) * OBS_ROWS, :]


def diffuse_body(steps_ref, in_ref, out_ref, buf, line):
    lat8 = LAT // 8
    for a in range(lat8):
        for j in range(LINE):
            buf[0, a, :, j * LANES : (j + 1) * LANES] = in_ref[pl.ds(a * line + j, 8, stride=8 * line), :]
    sub = lax.broadcasted_iota(I32, (8, LANES), 0)
    lane = lanes8()

    def step(k, carry):
        now, later = lax.rem(k, 2), lax.rem(k + 1, 2)
        old_right, cur = None, None
        for a in range(lat8):
            right = {}
            left = {}

            def tile(aa, j):
                return buf[now, aa, :, j * LANES : (j + 1) * LANES]

            x = [tile(a, j) for j in range(LINE)]
            right = [pltpu.roll(v, 1, 1) for v in x]
            left = [pltpu.roll(v, LANES - 1, 1) for v in x]
            for j in range(LINE):
                west = jnp.where(lane == 0, right[j - 1], right[j])
                east = jnp.where(lane == LANES - 1, left[(j + 1) % LINE], left[j])
                if a == 0:
                    north = jnp.where(sub == 0, 0.0, pltpu.roll(tile(lat8 - 1, j), 1, 0))
                else:
                    north = tile(a - 1, j)
                if a == lat8 - 1:
                    south = jnp.where(sub == 7, 0.0, pltpu.roll(tile(0, j), 7, 0))
                else:
                    south = tile(a + 1, j)
                laplace = ((north + south) + (west + east)) - 4.0 * x[j]
                buf[later, a, :, j * LANES : (j + 1) * LANES] = x[j] + 0.2 * laplace
        return carry

    count = steps_ref[0]
    lax.fori_loop(0, count, step, 0)
    end = lax.rem(count, 2)
    for a in range(lat8):
        for j in range(LINE):
            out_ref[pl.ds(a * LINE + j, 8, stride=8 * LINE), :] = buf[end, a, :, j * LANES : (j + 1) * LANES]


def diffuse_first_kernel(steps_ref, in_ref, out_ref, value_ref, var_ref, buf):
    diffuse_body(steps_ref, in_ref, out_ref, buf, LINE_OBS)
    for t in range(TILES):
        for r, ref in enumerate((value_ref, var_ref)):
            at = (t * 2 + r) * LINE_OBS + LINE
            ref[t * OBS_ROWS : (t + 1) * OBS_ROWS, :] = in_ref[at : at + OBS_ROWS, :]


def diffuse_kernel(steps_ref, in_ref, out_ref, buf):
    diffuse_body(steps_ref, in_ref, out_ref, buf, LINE)


def slots_kernel(index_ref, weight_ref, out_ref):
    def body(s, carry):
        index = index_ref[s]
        weight = weight_ref[s]
        at = index.astype(F32) + 0.5
        chan = jnp.floor(at * (1.0 / (ROWS * LON)))
        rest = at - chan * (ROWS * LON)
        below = rest > LON
        col = jnp.where(below, rest - LON, rest) - 0.5
        low, high = jnp.min(col, 0, keepdims=True), jnp.max(col, 0, keepdims=True)
        base = jnp.where(high - low > 1.5, high, low)
        chunk = jnp.floor((base + 0.5) * (1.0 / CHUNK))
        first = col == base
        rows = [chunk * CH + chan[0:1], base - chunk * CHUNK]
        for row in (jnp.logical_not(below), below):
            for column in (first, jnp.logical_not(first)):
                rows.append(jnp.sum(jnp.where(row & column, weight, 0.0), 0, keepdims=True))
        for k, row in enumerate(rows):
            out_ref[s, k : k + 1, :] = row
        return carry

    lax.fori_loop(0, TILES, body, 0)


def live_blocks(count_ref, list_ref, pad):
    def body(s, n):
        for j in range(PER_SRC):
            list_ref[n + j] = s * PER_SRC + j
        return n + lax.div(count_ref[s] + (BLOCK - 1), BLOCK)

    n = lax.fori_loop(0, TILES, body, 0)
    for j in range(pad):
        list_ref[n + j] = 0
    return n


def slot_rows(slot_ref, b):
    s = lax.div(b, PER_SRC)
    at = pl.multiple_of(lax.rem(b, PER_SRC) * BLOCK, BLOCK)
    return [slot_ref[s, k : k + 1, pl.ds(at, BLOCK)] for k in range(6)]


def one_hot(high):
    rows = lax.broadcasted_iota(I32, (HI, BLOCK), 0).astype(F32).astype(BF16)
    return jnp.where(rows == high.astype(BF16), jnp.ones((), BF16), jnp.zeros((), BF16))


def split(x):
    high = x.astype(BF16)
    return high, (x - high.astype(F32)).astype(BF16)


UNROLL = 2


def observe_kernel(scale, count_ref, got_ref, ens_ref, slot_ref, out_ref, inc_ref, table_ref, list_ref):
    for t in range(COLS):
        total = [jnp.zeros((8, LANES), F32) for f in range(FLD)]
        for m in range(GROUP):
            local = unpack_tile(got_ref, m, t, {})
            for pair in range(FLD // 2):
                ens = ens_ref[m, pair, :, t * LANES : (t + 1) * LANES].astype(F32)
                total[2 * pair] += ens[:8] * local
                total[2 * pair + 1] += ens[8:] * local
        for f in range(FLD):
            inc_ref[t, f * 8 : f * 8 + 8, :] = total[f] * scale
    for q in range(CHUNKS):
        for f in range(FLD):

            def where_from(lane):
                if lane > CHUNK:
                    return None
                col = (q * CHUNK + lane) % LON
                return (0, col // LANES, col % LANES)

            tile = assemble(lambda key, t: inc_ref[t, f * 8 : f * 8 + 8, :], where_from, {})
            table_ref[q * 32 + f * 8 : q * 32 + f * 8 + 8, :] = tile
    parts = []
    for r in range(ROWS):
        turned = table_ref[pl.ds(r, HI, stride=2), :].T
        parts.append(split(turned[:LO]))
    left = jnp.concatenate([parts[0][0], parts[1][0], parts[0][1], parts[1][1]], 0)

    out_ref[...] = jnp.zeros_like(out_ref)
    n = live_blocks(count_ref, list_ref, UNROLL)
    columns = lax.broadcasted_iota(I32, (LO, BLOCK), 0).astype(F32)

    def body(i, carry):
        for u in range(UNROLL):
            b = list_ref[i * UNROLL + u]
            high, low, w00, w01, w10, w11 = slot_rows(slot_ref, b)
            picked = jnp.dot(left, one_hot(high), preferred_element_type=F32)
            both = picked[: 2 * LO] + picked[2 * LO :]
            here, after = columns == low, columns == low + 1.0
            value = jnp.where(here, w00, jnp.where(after, w01, 0.0)) * both[:LO]
            value += jnp.where(here, w10, jnp.where(after, w11, 0.0)) * both[LO:]
            value = jnp.sum(value, 0, keepdims=True)
            for h in range(BLOCK // LANES):
                out_ref[pl.ds(b * (BLOCK // LANES) + h, 1), :] = value[:, h * LANES : (h + 1) * LANES]
        return carry

    lax.fori_loop(0, lax.div(n + UNROLL - 1, UNROLL), body, 0)


def adjoint_kernel(scale, count_ref, m0, m1, m2, m3, value_ref, var_ref, slot_ref, ens_ref, out_ref, dep_ref, acc_ref,
                   table_ref, adj_ref, proj_ref, list_ref):
    slot_at = lax.broadcasted_iota(I32, (OBS_ROWS, LANES), 0) * LANES + lax.broadcasted_iota(I32, (OBS_ROWS, LANES), 1)
    for s in range(TILES):
        at = slice(s * OBS_ROWS, (s + 1) * OBS_ROWS)
        model = (m0[at, :] + m1[at, :]) + (m2[at, :] + m3[at, :])
        weighted = var_ref[at, :] * (value_ref[at, :] - model)
        dep_ref[at, :] = jnp.where(slot_at < count_ref[s], weighted, 0.0)
    acc_ref[...] = jnp.zeros_like(acc_ref)
    n = live_blocks(count_ref, list_ref, UNROLL)
    columns = lax.broadcasted_iota(I32, (LO, BLOCK), 0).astype(F32).astype(BF16)

    def body(i, carry):
        total = acc_ref[...]
        for u in range(UNROLL):
            at = i * UNROLL + u
            b = list_ref[at]
            live = (at < n).astype(F32)
            high, low, w00, w01, w10, w11 = slot_rows(slot_ref, b)
            per = BLOCK // LANES
            dep = jnp.concatenate([dep_ref[pl.ds(b * per + h, 1), :] for h in range(per)], 1) * live
            here, after = columns == low.astype(BF16), columns == (low + 1.0).astype(BF16)
            halves = []
            for first, second in ((w00, w01), (w10, w11)):
                first, second = split(first * dep), split(second * dep)
                zero = jnp.zeros((), BF16)
                halves.append([jnp.where(here, x, jnp.where(after, y, zero)) for x, y in zip(first, second)])
            spread = jnp.concatenate([halves[0][0], halves[1][0], halves[0][1], halves[1][1]], 0)
            total += lax.dot_general(spread, one_hot(high), (((1,), (1,)), ((), ())), preferred_element_type=F32)
        acc_ref[...] = total
        return carry

    lax.fori_loop(0, lax.div(n + UNROLL - 1, UNROLL), body, 0)
    both = acc_ref[: 2 * LO, :] + acc_ref[2 * LO :, :]
    for r in range(ROWS):
        part = jnp.concatenate([both[r * LO : (r + 1) * LO], jnp.zeros((LANES - LO, HI), F32)], 0)
        table_ref[pl.ds(r, HI, stride=2), :] = part.T * scale
    lane = lanes8()
    for f in range(FLD):
        for t in range(COLS):
            total = jnp.zeros((8, LANES), F32)
            for q in range(-1, CHUNKS):
                first, last = max(q * CHUNK, t * LANES), min(q * CHUNK + CHUNK, t * LANES + LANES - 1, LON - 1)
                if first > last:
                    continue
                chunk = table_ref[(q % CHUNKS) * 32 + f * 8 : (q % CHUNKS) * 32 + f * 8 + 8, :]
                shift = (q * CHUNK - t * LANES) % LANES
                chunk = pltpu.roll(chunk, shift, 1) if shift else chunk
                mask = (lane >= first - t * LANES) & (lane <= last - t * LANES)
                total += jnp.where(mask, chunk, 0.0)
            adj_ref[t, f * 8 : f * 8 + 8, :] = total
    for t in range(COLS):
        adj = [adj_ref[t, f * 8 : f * 8 + 8, :] for f in range(FLD)]
        for m in range(GROUP):
            total = jnp.zeros((8, LANES), F32)
            for pair in range(FLD // 2):
                ens = ens_ref[m, pair, :, t * LANES : (t + 1) * LANES].astype(F32)
                total += ens[:8] * adj[2 * pair] + ens[8:] * adj[2 * pair + 1]
            proj_ref[t, m * 8 : m * 8 + 8, :] = total

    def store(row, tile):
        out_ref[pl.ds(row, 8, stride=LINE), :] = tile

    pack_rows(lambda m, t: proj_ref[t, m * 8 : m * 8 + 8, :], store, LINE)


def gradient_kernel(alpha_ref, got_ref, out_ref):
    for m in range(GROUP):
        cache = {}
        for t in range(COLS):
            width = min(LANES, LON - t * LANES)
            tile = unpack_tile(got_ref, m, t, cache)
            at = (slice(m * 8, m * 8 + 8), slice(t * LANES, t * LANES + width))
            out_ref[at] = alpha_ref[at] - tile[:, :width]


def shape(*dims, dtype=F32):
    return jax.ShapeDtypeStruct(dims, dtype)


def exchange(x):
    return lax.all_to_all(x, "tile", 0, 0, tiled=True)


def shards(alpha, ensemble, step_count, obs_index, obs_weight, obs_count, obs_value, inv_var):
    members = GROUP * lax.axis_size("member")
    scale = 1.0 / math.sqrt(members - 1)
    me = lax.axis_index("tile")
    steps = lax.dynamic_slice(step_count, (lax.rem(me, LEV),), (1,))
    counts = obs_count[0]
    wide = ((0, 0), (0, COLS * LANES - LON))
    rows = jnp.pad(alpha.reshape(GROUP * 8, LON), wide)
    ens = jnp.pad(ensemble.reshape(GROUP, 2, 16, LON), ((0, 0), (0, 0)) + wide)
    value = obs_value.reshape(TILES * OBS_ROWS, LANES)
    var = inv_var.reshape(TILES * OBS_ROWS, LANES)
    flat = shape(TILES * OBS_ROWS, LANES)

    sent = pl.pallas_call(
        pack_kernel,
        out_shape=shape(LAT * LINE_OBS, LANES),
        in_specs=[VMEM] * 3,
        out_specs=VMEM,
        compiler_params=params(16),
        name="pack",
    )(rows, value, var)
    got = exchange(sent)

    slots = pl.pallas_call(
        slots_kernel,
        out_shape=shape(TILES, 8, SLOT),
        in_specs=[VMEM] * 2,
        out_specs=VMEM,
        compiler_params=params(16),
        cost_estimate=pl.CostEstimate(flops=8000000, bytes_accessed=2097152, transcendentals=0),
        name="slots",
    )(obs_index[0], obs_weight[0])

    buf = pltpu.VMEM((2, 8, 8, LINE * LANES), F32)
    moved, value, var = pl.pallas_call(
        diffuse_first_kernel,
        out_shape=(shape(LAT * LINE, LANES), flat, flat),
        in_specs=[SMEM, VMEM],
        out_specs=[VMEM] * 3,
        scratch_shapes=[buf],
        compiler_params=params(16),
        name="diffuse_first",
    )(steps, got)
    got = exchange(moved)

    block_list = pltpu.SMEM((BLOCKS + 8,), I32)
    mine = pl.pallas_call(
        lambda *refs: observe_kernel(scale, *refs),
        out_shape=flat,
        in_specs=[SMEM] + [VMEM] * 3,
        out_specs=VMEM,
        scratch_shapes=[pltpu.VMEM((COLS, 32, LANES), F32), pltpu.VMEM((2 * HI, LANES), F32), block_list],
        compiler_params=params(16),
        name="observe",
    )(counts, got, ens, slots)
    others = [lax.ppermute(mine, "member", [(i, (i + k) % 4) for i in range(4)]) for k in (1, 3, 2)]

    sent, departure = pl.pallas_call(
        lambda *refs: adjoint_kernel(scale, *refs),
        out_shape=(shape(LAT * LINE, LANES), flat),
        in_specs=[SMEM] + [VMEM] * 8,
        out_specs=[VMEM] * 2,
        scratch_shapes=[
            pltpu.VMEM((4 * LO, HI), F32),
            pltpu.VMEM((2 * HI, LANES), F32),
            pltpu.VMEM((COLS, 32, LANES), F32),
            pltpu.VMEM((COLS, GROUP * 8, LANES), F32),
            block_list,
        ],
        compiler_params=params(20),
        name="adjoint",
    )(counts, mine, *others, value, var, slots, ens)
    got = exchange(sent)

    moved = pl.pallas_call(
        diffuse_kernel,
        out_shape=shape(LAT * LINE, LANES),
        in_specs=[SMEM, VMEM],
        out_specs=VMEM,
        scratch_shapes=[buf],
        compiler_params=params(16),
        name="diffuse",
    )(steps, got)
    got = exchange(moved)

    gradient = pl.pallas_call(
        gradient_kernel,
        out_shape=shape(GROUP * 8, LON),
        in_specs=[VMEM] * 2,
        out_specs=VMEM,
        compiler_params=params(16),
        name="gradient",
    )(rows, got)
    return gradient.reshape(alpha.shape), departure.reshape(1, TILES, SLOT)


def solution(mesh):
    return jax.shard_map(
        shards,
        mesh=mesh,
        in_specs=(
            P("member", None, "tile", None),
            P("member", None, None, "tile", None),
            P(),
            P("tile", None, None, None),
            P("tile", None, None, None),
            P("tile", None),
            P(None, "tile", None),
            P(None, "tile", None),
        ),
        out_specs=(P("member", None, "tile", None), P("tile", None, None)),
        check_vma=False,
    )
```

```python
import math

import jax
import jax.numpy as jnp
from jax import lax
from jax.experimental import pallas as pl
from jax.experimental.pallas import tpu as pltpu
from jax.sharding import PartitionSpec as P

FLD, LEV, ROWS, LON = 4, 4, 2, 1440
TILES, SLOT, GROUP = 32, 1024, 20
LAT = TILES * ROWS
CH = FLD * LEV
KMAX = 8

PIECES = 5
MGRP = GROUP // PIECES
HALF = LON // 2
PIECE = HALF + 2 * KMAX
LANES = 128
LINE = -(-PIECES * PIECE // LANES)
COLS = -(-LON // LANES)
OBS_ROWS = SLOT // LANES
EARLY = OBS_ROWS - 1
THERE, BACK = LINE + EARLY, 32

CHUNK = 90
CHUNKS = LON // CHUNK
HI = CH * CHUNKS
LO = 96
BLOCK = 256
BLOCKS = TILES * OBS_ROWS

F32, BF16, I32 = jnp.float32, jnp.bfloat16, jnp.int32
VMEM = pl.BlockSpec(memory_space=pltpu.VMEM)
SMEM = pl.BlockSpec(memory_space=pltpu.SMEM)


def params(mib):
    return pltpu.CompilerParams(vmem_limit_bytes=mib * 1024 * 1024)


def lanes8():
    return lax.broadcasted_iota(I32, (8, LANES), 1)


def assemble(fetch, where_from, cache):
    value, start, last = None, 0, None
    segments = []
    for lane in range(LANES):
        src = where_from(lane)
        if src is None:
            continue
        key, tile, at = src
        this = (key, tile, (lane - at) % LANES)
        if this != last:
            segments.append((lane, this))
            last = this
    for start, (key, tile, shift) in segments:
        if (key, tile, shift) not in cache:
            x = fetch(key, tile)
            cache[key, tile, shift] = pltpu.roll(x, shift, 1) if shift else x
        x = cache[key, tile, shift]
        value = x if value is None else jnp.where(lanes8() >= start, x, value)
    return value


def pack_rows(fetch, store, line):
    for mgrp in range(MGRP):
        for half in range(2):
            cache = {}
            for j in range(LINE):

                def where_from(lane):
                    piece, at = divmod(j * LANES + lane, PIECE)
                    if piece >= PIECES:
                        return None
                    col = (at - KMAX + half * HALF) % LON
                    return (piece, col // LANES, col % LANES)

                tile = assemble(lambda piece, t: fetch(piece * MGRP + mgrp, t), where_from, cache)
                store((half * MGRP * 8 + mgrp * 8) * line + j, tile)


def unpack_tile(got_ref, member, t, cache):
    piece, mgrp = divmod(member, MGRP)

    def where_from(lane):
        col = t * LANES + lane
        if col >= LON:
            return None
        half, at = divmod(col, HALF)
        at += piece * PIECE + KMAX
        return (half, at // LANES, at % LANES)

    def fetch(half, j):
        return got_ref[pl.ds((half * MGRP * 8 + mgrp * 8) * BACK + j, 8, stride=BACK), :]

    return assemble(fetch, where_from, cache)


def pack_kernel(alpha_ref, value_ref, var_ref, out_ref):
    def fetch(member, t):
        return alpha_ref[member * 8 : member * 8 + 8, t * LANES : (t + 1) * LANES]

    def store(row, tile):
        out_ref[pl.ds(row, 8, stride=THERE), :] = tile

    pack_rows(fetch, store, THERE)
    for d in range(TILES):
        for r, ref in enumerate((value_ref, var_ref)):
            at = (d * 2 + r) * THERE + LINE
            out_ref[at : at + EARLY, :] = ref[d * OBS_ROWS : d * OBS_ROWS + EARLY, :]


def diffuse_body(steps_ref, in_ref, out_ref, buf, line):
    lat8 = LAT // 8
    for j in range(LINE):
        for a in range(lat8):
            buf[0, j, a] = in_ref[pl.ds(a * line + j, 8, stride=8 * line), :]
    sub = lax.broadcasted_iota(I32, (8, LANES), 0)
    lane = lanes8()

    def step(k, carry):
        now, later = lax.rem(k, 2), lax.rem(k + 1, 2)

        def column(j):
            return [buf[now, j % LINE, a] for a in range(lat8)]

        def turn(column, by):
            return [pltpu.roll(v, by, 1) for v in column]

        before = turn(column(LINE - 1), 1)
        x = column(0)
        left = turn(x, LANES - 1)
        for j in range(LINE):
            ahead = column(j + 1)
            right = turn(x, 1)
            after = turn(ahead, LANES - 1)
            for a in range(lat8):
                west = jnp.where(lane == 0, before[a], right[a])
                east = jnp.where(lane == LANES - 1, after[a], left[a])
                north = x[a - 1] if a else jnp.where(sub == 0, 0.0, pltpu.roll(x[lat8 - 1], 1, 0))
                south = x[a + 1] if a < lat8 - 1 else jnp.where(sub == 7, 0.0, pltpu.roll(x[0], 7, 0))
                buf[later, j, a] = 0.2 * ((north + south) + (west + east)) + (1.0 - 4.0 * 0.2) * x[a]
            before, x, left = right, ahead, after
        return carry

    count = steps_ref[0]
    lax.fori_loop(0, count, step, 0)
    end = lax.rem(count, 2)
    for j in range(LINE):
        for a in range(lat8):
            out_ref[pl.ds(a * BACK + j, 8, stride=8 * BACK), :] = buf[end, j, a]


def diffuse_first_kernel(steps_ref, in_ref, own_value_ref, own_var_ref, out_ref, value_ref, var_ref, buf):
    diffuse_body(steps_ref, in_ref, out_ref, buf, THERE)
    for r, (own_ref, ref) in enumerate(((own_value_ref, value_ref), (own_var_ref, var_ref))):
        for t in range(TILES):
            at = (t * 2 + r) * THERE + LINE
            ref[t * OBS_ROWS : t * OBS_ROWS + EARLY, :] = in_ref[at : at + EARLY, :]
        for t in range(0, TILES, 8):
            late = own_ref[pl.ds(t * OBS_ROWS + EARLY, 8, stride=OBS_ROWS), :]
            out_ref[pl.ds((t * 2 + r) * BACK + LINE, 8, stride=2 * BACK), :] = late


def diffuse_kernel(steps_ref, in_ref, out_ref, buf):
    diffuse_body(steps_ref, in_ref, out_ref, buf, BACK)


def slots_kernel(index_ref, weight_ref, out_ref):
    def body(s, carry):
        index = index_ref[s]
        weight = weight_ref[s]
        at = index.astype(F32) + 0.5
        chan = jnp.floor(at * (1.0 / (ROWS * LON)))
        rest = at - chan * (ROWS * LON)
        below = rest > LON
        col = jnp.where(below, rest - LON, rest) - 0.5
        low, high = jnp.min(col, 0, keepdims=True), jnp.max(col, 0, keepdims=True)
        base = jnp.where(high - low > 1.5, high, low)
        chunk = jnp.floor((base + 0.5) * (1.0 / CHUNK))
        first = col == base
        rows = [chunk * CH + chan[0:1], base - chunk * CHUNK]
        for row in (jnp.logical_not(below), below):
            for column in (first, jnp.logical_not(first)):
                rows.append(jnp.sum(jnp.where(row & column, weight, 0.0), 0, keepdims=True))
        for k, row in enumerate(rows):
            for j in range(OBS_ROWS):
                out_ref[s * OBS_ROWS + j, k : k + 1, :] = row[:, j * LANES : (j + 1) * LANES]
        return carry

    lax.fori_loop(0, TILES, body, 0)


def live_blocks(count_ref, list_ref):
    def body(s, n):
        for j in range(OBS_ROWS):
            list_ref[n + j] = s * OBS_ROWS + j
        return n + lax.div(count_ref[s] + (LANES - 1), LANES)

    n = lax.fori_loop(0, TILES, body, 0)
    for j in range(2 * FEW):
        list_ref[n + j] = 0
    return n


def over_live(n, body):
    many = lax.div(n, 2 * MANY)
    done = many * (2 * MANY)

    def large(i, carry):
        body(i * (2 * MANY), MANY)
        return carry

    def small(i, carry):
        body(done + i * (2 * FEW), FEW)
        return carry

    lax.fori_loop(0, many, large, 0)
    lax.fori_loop(0, lax.div(n - done + (2 * FEW - 1), 2 * FEW), small, 0)


def slot_rows(slot_ref, pair):
    blocks = [slot_ref[b] for b in pair]
    return [jnp.concatenate([x[k : k + 1] for x in blocks], 1) for k in range(6)]


def one_hot(high):
    rows = lax.broadcasted_iota(I32, (HI, BLOCK), 0).astype(F32).astype(BF16)
    return jnp.where(rows == high.astype(BF16), jnp.ones((), BF16), jnp.zeros((), BF16))


def split(x):
    high = x.astype(BF16)
    return high, (x - high.astype(F32)).astype(BF16)


MANY, FEW = 8, 2


def observe_kernel(scale, count_ref, got_ref, ens_ref, slot_ref, out_ref, inc_ref, table_ref, list_ref):
    for t in range(COLS):
        total = [jnp.zeros((8, LANES), F32) for f in range(FLD)]
        for m in range(GROUP):
            local = unpack_tile(got_ref, m, t, {})
            for pair in range(FLD // 2):
                ens = ens_ref[m, pair, :, t * LANES : (t + 1) * LANES].astype(F32)
                total[2 * pair] += ens[:8] * local
                total[2 * pair + 1] += ens[8:] * local
        for f in range(FLD):
            inc_ref[t, f * 8 : f * 8 + 8, :] = total[f] * scale
    for q in range(CHUNKS):
        for f in range(FLD):

            def where_from(lane):
                if lane > CHUNK:
                    return None
                col = (q * CHUNK + lane) % LON
                return (0, col // LANES, col % LANES)

            tile = assemble(lambda key, t: inc_ref[t, f * 8 : f * 8 + 8, :], where_from, {})
            table_ref[q * 32 + f * 8 : q * 32 + f * 8 + 8, :] = tile
    parts = []
    for r in range(ROWS):
        turned = table_ref[pl.ds(r, HI, stride=2), :].T
        parts.append(split(turned[:LO]))
    left = jnp.concatenate([parts[0][0], parts[1][0], parts[0][1], parts[1][1]], 0)

    out_ref[...] = jnp.zeros_like(out_ref)
    n = live_blocks(count_ref, list_ref)
    columns = lax.broadcasted_iota(I32, (LO, BLOCK), 0).astype(F32)

    def body(start, pairs):
        for u in range(pairs):
            pair = [list_ref[start + 2 * u + h] for h in range(2)]
            high, low, w00, w01, w10, w11 = slot_rows(slot_ref, pair)
            picked = jnp.dot(left, one_hot(high), preferred_element_type=F32)
            both = picked[: 2 * LO] + picked[2 * LO :]
            here, after = columns == low, columns == low + 1.0
            value = jnp.where(here, w00, jnp.where(after, w01, 0.0)) * both[:LO]
            value += jnp.where(here, w10, jnp.where(after, w11, 0.0)) * both[LO:]
            value = jnp.sum(value, 0, keepdims=True)
            for h in range(2):
                out_ref[pl.ds(pair[h], 1), :] = value[:, h * LANES : (h + 1) * LANES]

    over_live(n, body)


def adjoint_kernel(scale, count_ref, m0, m1, m2, m3, value_ref, var_ref, late_ref, slot_ref, ens_ref, out_ref, dep_ref,
                   acc_ref, table_ref, adj_ref, proj_ref, list_ref):
    slot_at = lax.broadcasted_iota(I32, (OBS_ROWS, LANES), 0) * LANES + lax.broadcasted_iota(I32, (OBS_ROWS, LANES), 1)
    last = slot_at >= EARLY * LANES
    for s in range(TILES):
        at = slice(s * OBS_ROWS, (s + 1) * OBS_ROWS)
        model = (m0[at, :] + m1[at, :]) + (m2[at, :] + m3[at, :])
        late = [late_ref[(s * 2 + r) * BACK + LINE : (s * 2 + r) * BACK + LINE + 1, :] for r in range(2)]
        value, var = (jnp.where(last, x, ref[at, :]) for x, ref in zip(late, (value_ref, var_ref)))
        weighted = var * (value - model)
        dep_ref[at, :] = jnp.where(slot_at < count_ref[s], weighted, 0.0)
    acc_ref[...] = jnp.zeros_like(acc_ref)
    n = live_blocks(count_ref, list_ref)
    columns = lax.broadcasted_iota(I32, (LO, BLOCK), 0).astype(F32).astype(BF16)

    def body(start, pairs):
        spreads, hots = [], []
        for u in range(pairs):
            at = [start + 2 * u + h for h in range(2)]
            pair = [list_ref[k] for k in at]
            high, low, w00, w01, w10, w11 = slot_rows(slot_ref, pair)
            dep = [jnp.where(k < n, dep_ref[pl.ds(b, 1), :], 0.0) for k, b in zip(at, pair)]
            dep = jnp.concatenate(dep, 1)
            here, after = columns == low.astype(BF16), columns == (low + 1.0).astype(BF16)
            halves = []
            for first, second in ((w00, w01), (w10, w11)):
                first, second = split(first * dep), split(second * dep)
                zero = jnp.zeros((), BF16)
                halves.append([jnp.where(here, x, jnp.where(after, y, zero)) for x, y in zip(first, second)])
            spreads.append(jnp.concatenate([halves[0][0], halves[1][0], halves[0][1], halves[1][1]], 0))
            hots.append(one_hot(high))
        spread, hot = jnp.concatenate(spreads, 1), jnp.concatenate(hots, 1)
        acc_ref[...] += lax.dot_general(spread, hot, (((1,), (1,)), ((), ())), preferred_element_type=F32)

    over_live(n, body)
    both = acc_ref[: 2 * LO, :] + acc_ref[2 * LO :, :]
    for r in range(ROWS):
        part = jnp.concatenate([both[r * LO : (r + 1) * LO], jnp.zeros((LANES - LO, HI), F32)], 0)
        table_ref[pl.ds(r, HI, stride=2), :] = part.T * scale
    lane = lanes8()
    for f in range(FLD):
        for t in range(COLS):
            total = jnp.zeros((8, LANES), F32)
            for q in range(-1, CHUNKS):
                first, last = max(q * CHUNK, t * LANES), min(q * CHUNK + CHUNK, t * LANES + LANES - 1, LON - 1)
                if first > last:
                    continue
                chunk = table_ref[(q % CHUNKS) * 32 + f * 8 : (q % CHUNKS) * 32 + f * 8 + 8, :]
                shift = (q * CHUNK - t * LANES) % LANES
                chunk = pltpu.roll(chunk, shift, 1) if shift else chunk
                mask = (lane >= first - t * LANES) & (lane <= last - t * LANES)
                total += jnp.where(mask, chunk, 0.0)
            adj_ref[t, f * 8 : f * 8 + 8, :] = total
    for t in range(COLS):
        adj = [adj_ref[t, f * 8 : f * 8 + 8, :] for f in range(FLD)]
        for m in range(GROUP):
            total = jnp.zeros((8, LANES), F32)
            for pair in range(FLD // 2):
                ens = ens_ref[m, pair, :, t * LANES : (t + 1) * LANES].astype(F32)
                total += ens[:8] * adj[2 * pair] + ens[8:] * adj[2 * pair + 1]
            proj_ref[t, m * 8 : m * 8 + 8, :] = total

    def store(row, tile):
        out_ref[pl.ds(row, 8, stride=BACK), :] = tile

    pack_rows(lambda m, t: proj_ref[t, m * 8 : m * 8 + 8, :], store, BACK)


def gradient_kernel(alpha_ref, got_ref, out_ref):
    for m in range(GROUP):
        cache = {}
        for t in range(COLS):
            width = min(LANES, LON - t * LANES)
            tile = unpack_tile(got_ref, m, t, cache)
            at = (slice(m * 8, m * 8 + 8), slice(t * LANES, t * LANES + width))
            out_ref[at] = alpha_ref[at] - tile[:, :width]


def shape(*dims, dtype=F32):
    return jax.ShapeDtypeStruct(dims, dtype)


def exchange(x):
    return lax.all_to_all(x, "tile", 0, 0, tiled=True)


def shards(alpha, ensemble, step_count, obs_index, obs_weight, obs_count, obs_value, inv_var):
    members = GROUP * lax.axis_size("member")
    scale = 1.0 / math.sqrt(members - 1)
    me = lax.axis_index("tile")
    steps = lax.dynamic_slice(step_count, (lax.rem(me, LEV),), (1,))
    counts = obs_count[0]
    wide = ((0, 0), (0, COLS * LANES - LON))
    rows = jnp.pad(alpha.reshape(GROUP * 8, LON), wide)
    ens = jnp.pad(ensemble.reshape(GROUP, 2, 16, LON), ((0, 0), (0, 0)) + wide)
    value = obs_value.reshape(TILES * OBS_ROWS, LANES)
    var = inv_var.reshape(TILES * OBS_ROWS, LANES)
    flat = shape(TILES * OBS_ROWS, LANES)

    sent = pl.pallas_call(
        pack_kernel,
        out_shape=shape(LAT * THERE, LANES),
        in_specs=[VMEM] * 3,
        out_specs=VMEM,
        compiler_params=params(16),
        name="pack",
    )(rows, value, var)
    got = exchange(sent)

    slots = pl.pallas_call(
        slots_kernel,
        out_shape=shape(BLOCKS, 8, LANES),
        in_specs=[VMEM] * 2,
        out_specs=VMEM,
        compiler_params=params(16),
        cost_estimate=pl.CostEstimate(flops=8000000, bytes_accessed=2097152, transcendentals=0),
        name="slots",
    )(obs_index[0], obs_weight[0])

    buf = pltpu.VMEM((2, LINE, 8, 8, LANES), F32)
    moved, value, var = pl.pallas_call(
        diffuse_first_kernel,
        out_shape=(shape(LAT * BACK, LANES), flat, flat),
        in_specs=[SMEM] + [VMEM] * 3,
        out_specs=[VMEM] * 3,
        scratch_shapes=[buf],
        compiler_params=params(16),
        name="diffuse_first",
    )(steps, got, value, var)
    got = exchange(moved)

    block_list = pltpu.SMEM((BLOCKS + 8,), I32)
    mine = pl.pallas_call(
        lambda *refs: observe_kernel(scale, *refs),
        out_shape=flat,
        in_specs=[SMEM] + [VMEM] * 3,
        out_specs=VMEM,
        scratch_shapes=[pltpu.VMEM((COLS, 32, LANES), F32), pltpu.VMEM((2 * HI, LANES), F32), block_list],
        compiler_params=params(16),
        name="observe",
    )(counts, got, ens, slots)
    others = [lax.ppermute(mine, "member", [(i, (i + k) % 4) for i in range(4)]) for k in (1, 3, 2)]

    sent, departure = pl.pallas_call(
        lambda *refs: adjoint_kernel(scale, *refs),
        out_shape=(shape(LAT * BACK, LANES), flat),
        in_specs=[SMEM] + [VMEM] * 9,
        out_specs=[VMEM] * 2,
        scratch_shapes=[
            pltpu.VMEM((4 * LO, HI), F32),
            pltpu.VMEM((2 * HI, LANES), F32),
            pltpu.VMEM((COLS, 32, LANES), F32),
            pltpu.VMEM((COLS, GROUP * 8, LANES), F32),
            block_list,
        ],
        compiler_params=params(24),
        name="adjoint",
    )(counts, mine, *others, value, var, got, slots, ens)
    got = exchange(sent)

    moved = pl.pallas_call(
        diffuse_kernel,
        out_shape=shape(LAT * BACK, LANES),
        in_specs=[SMEM, VMEM],
        out_specs=VMEM,
        scratch_shapes=[buf],
        compiler_params=params(16),
        name="diffuse",
    )(steps, got)
    got = exchange(moved)

    gradient = pl.pallas_call(
        gradient_kernel,
        out_shape=shape(GROUP * 8, LON),
        in_specs=[VMEM] * 2,
        out_specs=VMEM,
        compiler_params=params(16),
        name="gradient",
    )(rows, got)
    return gradient.reshape(alpha.shape), departure.reshape(1, TILES, SLOT)


def solution(mesh):
    return jax.shard_map(
        shards,
        mesh=mesh,
        in_specs=(
            P("member", None, "tile", None),
            P("member", None, None, "tile", None),
            P(),
            P("tile", None, None, None),
            P("tile", None, None, None),
            P("tile", None),
            P(None, "tile", None),
            P(None, "tile", None),
        ),
        out_specs=(P("member", None, "tile", None), P("tile", None, None)),
        check_vma=False,
    )
```

```python
import math

import jax
import jax.numpy as jnp
from jax import lax
from jax.experimental import pallas as pl
from jax.experimental.pallas import tpu as pltpu
from jax.sharding import PartitionSpec as P

FLD, LEV, ROWS, LON = 4, 4, 2, 1440
TILES, SLOT, GROUP = 32, 1024, 20
LAT = TILES * ROWS
CH = FLD * LEV
KMAX = 8

PIECES = 5
MGRP = GROUP // PIECES
HALF = LON // 2
PIECE = HALF + 2 * KMAX
LANES = 128
LINE = -(-PIECES * PIECE // LANES)
COLS = -(-LON // LANES)
OBS_ROWS = SLOT // LANES
THERE, BACK = LINE + OBS_ROWS, LINE
DEEP, WIDE = 16, 32

CHUNK = 90
CHUNKS = LON // CHUNK
HI = CH * CHUNKS
LO = 96
BLOCK = 256
BLOCKS = TILES * OBS_ROWS

F32, BF16, I32 = jnp.float32, jnp.bfloat16, jnp.int32
VMEM = pl.BlockSpec(memory_space=pltpu.VMEM)
SMEM = pl.BlockSpec(memory_space=pltpu.SMEM)


def params(mib):
    return pltpu.CompilerParams(vmem_limit_bytes=mib * 1024 * 1024)


def lanes8():
    return lax.broadcasted_iota(I32, (8, LANES), 1)


def assemble(fetch, where_from, cache):
    value, start, last = None, 0, None
    segments = []
    for lane in range(LANES):
        src = where_from(lane)
        if src is None:
            continue
        key, tile, at = src
        this = (key, tile, (lane - at) % LANES)
        if this != last:
            segments.append((lane, this))
            last = this
    for start, (key, tile, shift) in segments:
        if (key, tile, shift) not in cache:
            x = fetch(key, tile)
            cache[key, tile, shift] = pltpu.roll(x, shift, 1) if shift else x
        x = cache[key, tile, shift]
        value = x if value is None else jnp.where(lanes8() >= start, x, value)
    return value


def pack_rows(fetch, store, line):
    for mgrp in range(MGRP):
        for half in range(2):
            cache = {}
            for j in range(LINE):

                def where_from(lane):
                    piece, at = divmod(j * LANES + lane, PIECE)
                    if piece >= PIECES:
                        return None
                    col = (at - KMAX + half * HALF) % LON
                    return (piece, col // LANES, col % LANES)

                tile = assemble(lambda piece, t: fetch(piece * MGRP + mgrp, t), where_from, cache)
                store((half * MGRP * 8 + mgrp * 8) * line + j, tile)


def unpack_tile(got_ref, member, t, cache):
    piece, mgrp = divmod(member, MGRP)

    def where_from(lane):
        col = t * LANES + lane
        if col >= LON:
            return None
        half, at = divmod(col, HALF)
        at += piece * PIECE + KMAX
        return (half, at // LANES, at % LANES)

    def fetch(half, j):
        return got_ref[pl.ds((half * MGRP * 8 + mgrp * 8) * BACK + j, 8, stride=BACK), :]

    return assemble(fetch, where_from, cache)


def pack_kernel(alpha_ref, value_ref, var_ref, out_ref):
    def fetch(member, t):
        return alpha_ref[member * 8 : member * 8 + 8, t * LANES : (t + 1) * LANES]

    def store(row, tile):
        out_ref[pl.ds(row, 8, stride=THERE), :] = tile

    pack_rows(fetch, store, THERE)
    for d in range(TILES):
        for r, ref in enumerate((value_ref, var_ref)):
            at = (d * 2 + r) * THERE + LINE
            out_ref[at : at + OBS_ROWS, :] = ref[d * OBS_ROWS : (d + 1) * OBS_ROWS, :]


def diffuse_step(src, dst):
    sub = lax.broadcasted_iota(I32, (8, LANES), 0)
    lane = lanes8()

    def plane(g):
        return [src[g, a] for a in range(DEEP)]

    above = [jnp.where(lane < WIDE, 0.0, pltpu.roll(v, WIDE, 1)) for v in plane(DEEP - 1)]
    here = plane(0)
    for g in range(DEEP):
        if g < DEEP - 1:
            below = plane(g + 1)
        else:
            below = [jnp.where(lane >= LANES - WIDE, 0.0, pltpu.roll(v, LANES - WIDE, 1)) for v in plane(0)]
        west = pltpu.roll(here[-1], 1, 0)
        west = jnp.where(sub == 0, pltpu.roll(west, 1, 1), west)
        east = pltpu.roll(here[0], 7, 0)
        east = jnp.where(sub == 7, pltpu.roll(east, LANES - 1, 1), east)
        line = [west] + here + [east]
        for a in range(DEEP):
            near = (above[a] + below[a]) + (line[a] + line[a + 2])
            dst[g, a] = 0.2 * near + (1.0 - 4.0 * 0.2) * here[a]
        above, here = here, below


def diffuse_body(steps_ref, in_ref, out_ref, one, two, turned, line):
    blocks = LANES // WIDE
    for g in range(DEEP):
        lines = []
        for q in range(blocks):
            at = (DEEP * q + g) * line
            piece = in_ref[at : at + LINE, :]
            lines += [piece, jnp.zeros((WIDE - LINE, LANES), F32)]
        turned[g] = jnp.concatenate(lines, 0).T
    for g in range(DEEP):
        for a in range(DEEP):
            one[g, a] = turned[g, pl.ds(a, 8, stride=DEEP), :]
    count = steps_ref[0]

    def pair(k, carry):
        diffuse_step(one, two)
        diffuse_step(two, one)
        return carry

    lax.fori_loop(0, lax.div(count, 2), pair, 0)

    def put(src):
        for g in range(DEEP):
            for a in range(DEEP):
                turned[g, pl.ds(a, 8, stride=DEEP), :] = src[g, a]
        for g in range(DEEP):
            lines = turned[g].T
            for q in range(blocks):
                at = (DEEP * q + g) * BACK
                out_ref[at : at + LINE, :] = lines[q * WIDE : q * WIDE + LINE]

    odd = lax.rem(count, 2)

    @pl.when(odd == 1)
    def _():
        diffuse_step(one, two)
        put(two)

    @pl.when(odd == 0)
    def _():
        put(one)


def diffuse_first_kernel(steps_ref, in_ref, out_ref, value_ref, var_ref, one, two, turned):
    diffuse_body(steps_ref, in_ref, out_ref, one, two, turned, THERE)
    for t in range(TILES):
        for r, ref in enumerate((value_ref, var_ref)):
            at = (t * 2 + r) * THERE + LINE
            ref[t * OBS_ROWS : (t + 1) * OBS_ROWS, :] = in_ref[at : at + OBS_ROWS, :]


def diffuse_kernel(steps_ref, in_ref, out_ref, one, two, turned):
    diffuse_body(steps_ref, in_ref, out_ref, one, two, turned, BACK)


def slots_kernel(index_ref, weight_ref, out_ref):
    def body(s, carry):
        index = index_ref[s]
        weight = weight_ref[s]
        at = index.astype(F32) + 0.5
        chan = jnp.floor(at * (1.0 / (ROWS * LON)))
        rest = at - chan * (ROWS * LON)
        below = rest > LON
        col = jnp.where(below, rest - LON, rest) - 0.5
        low, high = jnp.min(col, 0, keepdims=True), jnp.max(col, 0, keepdims=True)
        base = jnp.where(high - low > 1.5, high, low)
        chunk = jnp.floor((base + 0.5) * (1.0 / CHUNK))
        first = col == base
        rows = [chunk * CH + chan[0:1], base - chunk * CHUNK]
        for row in (jnp.logical_not(below), below):
            for column in (first, jnp.logical_not(first)):
                rows.append(jnp.sum(jnp.where(row & column, weight, 0.0), 0, keepdims=True))
        for k, row in enumerate(rows):
            for j in range(OBS_ROWS):
                out_ref[s * OBS_ROWS + j, k : k + 1, :] = row[:, j * LANES : (j + 1) * LANES]
        return carry

    lax.fori_loop(0, TILES, body, 0)


def live_blocks(count_ref, list_ref):
    def body(s, n):
        for j in range(OBS_ROWS):
            list_ref[n + j] = s * OBS_ROWS + j
        return n + lax.div(count_ref[s] + (LANES - 1), LANES)

    n = lax.fori_loop(0, TILES, body, 0)
    for j in range(2 * FEW):
        list_ref[n + j] = 0
    return n


def over_live(n, body):
    many = lax.div(n, 2 * MANY)
    done = many * (2 * MANY)

    def large(i, carry):
        body(i * (2 * MANY), MANY)
        return carry

    def small(i, carry):
        body(done + i * (2 * FEW), FEW)
        return carry

    lax.fori_loop(0, many, large, 0)
    lax.fori_loop(0, lax.div(n - done + (2 * FEW - 1), 2 * FEW), small, 0)


def slot_rows(slot_ref, pair):
    blocks = [slot_ref[b] for b in pair]
    return [jnp.concatenate([x[k : k + 1] for x in blocks], 1) for k in range(6)]


def one_hot(high):
    rows = lax.broadcasted_iota(I32, (HI, BLOCK), 0).astype(F32).astype(BF16)
    return jnp.where(rows == high.astype(BF16), jnp.ones((), BF16), jnp.zeros((), BF16))


def split(x):
    high = x.astype(BF16)
    return high, (x - high.astype(F32)).astype(BF16)


MANY, FEW = 8, 2


def observe_kernel(scale, count_ref, got_ref, ens_ref, slot_ref, out_ref, inc_ref, table_ref, list_ref):
    for t in range(COLS):
        total = [jnp.zeros((8, LANES), F32) for f in range(FLD)]
        for m in range(GROUP):
            local = unpack_tile(got_ref, m, t, {})
            for pair in range(FLD // 2):
                ens = ens_ref[m, pair, :, t * LANES : (t + 1) * LANES].astype(F32)
                total[2 * pair] += ens[:8] * local
                total[2 * pair + 1] += ens[8:] * local
        for f in range(FLD):
            inc_ref[t, f * 8 : f * 8 + 8, :] = total[f] * scale
    for q in range(CHUNKS):
        for f in range(FLD):

            def where_from(lane):
                if lane > CHUNK:
                    return None
                col = (q * CHUNK + lane) % LON
                return (0, col // LANES, col % LANES)

            tile = assemble(lambda key, t: inc_ref[t, f * 8 : f * 8 + 8, :], where_from, {})
            table_ref[q * 32 + f * 8 : q * 32 + f * 8 + 8, :] = tile
    parts = []
    for r in range(ROWS):
        turned = table_ref[pl.ds(r, HI, stride=2), :].T
        parts.append(split(turned[:LO]))
    left = jnp.concatenate([parts[0][0], parts[1][0], parts[0][1], parts[1][1]], 0)

    out_ref[...] = jnp.zeros_like(out_ref)
    n = live_blocks(count_ref, list_ref)
    columns = lax.broadcasted_iota(I32, (LO, BLOCK), 0).astype(F32)

    def body(start, pairs):
        for u in range(pairs):
            pair = [list_ref[start + 2 * u + h] for h in range(2)]
            high, low, w00, w01, w10, w11 = slot_rows(slot_ref, pair)
            picked = jnp.dot(left, one_hot(high), preferred_element_type=F32)
            both = picked[: 2 * LO] + picked[2 * LO :]
            here, after = columns == low, columns == low + 1.0
            value = jnp.where(here, w00, jnp.where(after, w01, 0.0)) * both[:LO]
            value += jnp.where(here, w10, jnp.where(after, w11, 0.0)) * both[LO:]
            value = jnp.sum(value, 0, keepdims=True)
            for h in range(2):
                out_ref[pl.ds(pair[h], 1), :] = value[:, h * LANES : (h + 1) * LANES]

    over_live(n, body)


def adjoint_kernel(scale, count_ref, m0, m1, m2, m3, value_ref, var_ref, slot_ref, ens_ref, out_ref, dep_ref, acc_ref,
                   table_ref, adj_ref, proj_ref, list_ref):
    slot_at = lax.broadcasted_iota(I32, (OBS_ROWS, LANES), 0) * LANES + lax.broadcasted_iota(I32, (OBS_ROWS, LANES), 1)
    for s in range(TILES):
        at = slice(s * OBS_ROWS, (s + 1) * OBS_ROWS)
        model = (m0[at, :] + m1[at, :]) + (m2[at, :] + m3[at, :])
        weighted = var_ref[at, :] * (value_ref[at, :] - model)
        dep_ref[at, :] = jnp.where(slot_at < count_ref[s], weighted, 0.0)
    acc_ref[...] = jnp.zeros_like(acc_ref)
    n = live_blocks(count_ref, list_ref)
    columns = lax.broadcasted_iota(I32, (LO, BLOCK), 0).astype(F32).astype(BF16)

    def body(start, pairs):
        spreads, hots = [], []
        for u in range(pairs):
            at = [start + 2 * u + h for h in range(2)]
            pair = [list_ref[k] for k in at]
            high, low, w00, w01, w10, w11 = slot_rows(slot_ref, pair)
            dep = [jnp.where(k < n, dep_ref[pl.ds(b, 1), :], 0.0) for k, b in zip(at, pair)]
            dep = jnp.concatenate(dep, 1)
            here, after = columns == low.astype(BF16), columns == (low + 1.0).astype(BF16)
            halves = []
            for first, second in ((w00, w01), (w10, w11)):
                first, second = split(first * dep), split(second * dep)
                zero = jnp.zeros((), BF16)
                halves.append([jnp.where(here, x, jnp.where(after, y, zero)) for x, y in zip(first, second)])
            spreads.append(jnp.concatenate([halves[0][0], halves[1][0], halves[0][1], halves[1][1]], 0))
            hots.append(one_hot(high))
        spread, hot = jnp.concatenate(spreads, 1), jnp.concatenate(hots, 1)
        acc_ref[...] += lax.dot_general(spread, hot, (((1,), (1,)), ((), ())), preferred_element_type=F32)

    over_live(n, body)
    both = acc_ref[: 2 * LO, :] + acc_ref[2 * LO :, :]
    for r in range(ROWS):
        part = jnp.concatenate([both[r * LO : (r + 1) * LO], jnp.zeros((LANES - LO, HI), F32)], 0)
        table_ref[pl.ds(r, HI, stride=2), :] = part.T * scale
    lane = lanes8()
    for f in range(FLD):
        for t in range(COLS):
            total = jnp.zeros((8, LANES), F32)
            for q in range(-1, CHUNKS):
                first, last = max(q * CHUNK, t * LANES), min(q * CHUNK + CHUNK, t * LANES + LANES - 1, LON - 1)
                if first > last:
                    continue
                chunk = table_ref[(q % CHUNKS) * 32 + f * 8 : (q % CHUNKS) * 32 + f * 8 + 8, :]
                shift = (q * CHUNK - t * LANES) % LANES
                chunk = pltpu.roll(chunk, shift, 1) if shift else chunk
                mask = (lane >= first - t * LANES) & (lane <= last - t * LANES)
                total += jnp.where(mask, chunk, 0.0)
            adj_ref[t, f * 8 : f * 8 + 8, :] = total
    for t in range(COLS):
        adj = [adj_ref[t, f * 8 : f * 8 + 8, :] for f in range(FLD)]
        for m in range(GROUP):
            total = jnp.zeros((8, LANES), F32)
            for pair in range(FLD // 2):
                ens = ens_ref[m, pair, :, t * LANES : (t + 1) * LANES].astype(F32)
                total += ens[:8] * adj[2 * pair] + ens[8:] * adj[2 * pair + 1]
            proj_ref[t, m * 8 : m * 8 + 8, :] = total

    def store(row, tile):
        out_ref[pl.ds(row, 8, stride=BACK), :] = tile

    pack_rows(lambda m, t: proj_ref[t, m * 8 : m * 8 + 8, :], store, BACK)


def gradient_kernel(alpha_ref, got_ref, out_ref):
    for m in range(GROUP):
        cache = {}
        for t in range(COLS):
            width = min(LANES, LON - t * LANES)
            tile = unpack_tile(got_ref, m, t, cache)
            at = (slice(m * 8, m * 8 + 8), slice(t * LANES, t * LANES + width))
            out_ref[at] = alpha_ref[at] - tile[:, :width]


def shape(*dims, dtype=F32):
    return jax.ShapeDtypeStruct(dims, dtype)


def exchange(x):
    rows = x.shape[0] // TILES
    x = x.reshape(TILES, rows // 2, 2, LANES)
    return lax.all_to_all(x, "tile", 0, 0, tiled=True).reshape(TILES * rows, LANES)


def shards(alpha, ensemble, step_count, obs_index, obs_weight, obs_count, obs_value, inv_var):
    members = GROUP * lax.axis_size("member")
    scale = 1.0 / math.sqrt(members - 1)
    me = lax.axis_index("tile")
    steps = lax.dynamic_slice(step_count, (lax.rem(me, LEV),), (1,))
    counts = obs_count[0]
    wide = ((0, 0), (0, COLS * LANES - LON))
    rows = jnp.pad(alpha.reshape(GROUP * 8, LON), wide)
    ens = jnp.pad(ensemble.reshape(GROUP, 2, 16, LON), ((0, 0), (0, 0)) + wide)
    value = obs_value.reshape(TILES * OBS_ROWS, LANES)
    var = inv_var.reshape(TILES * OBS_ROWS, LANES)
    flat = shape(TILES * OBS_ROWS, LANES)

    sent = pl.pallas_call(
        pack_kernel,
        out_shape=shape(LAT * THERE, LANES),
        in_specs=[VMEM] * 3,
        out_specs=VMEM,
        compiler_params=params(16),
        name="pack",
    )(rows, value, var)
    got = exchange(sent)

    slots = pl.pallas_call(
        slots_kernel,
        out_shape=shape(BLOCKS, 8, LANES),
        in_specs=[VMEM] * 2,
        out_specs=VMEM,
        compiler_params=params(16),
        cost_estimate=pl.CostEstimate(flops=8000000, bytes_accessed=2097152, transcendentals=0),
        name="slots",
    )(obs_index[0], obs_weight[0])

    buf = [pltpu.VMEM((DEEP, DEEP, 8, LANES), F32)] * 2 + [pltpu.VMEM((DEEP, LANES, LANES), F32)]
    moved, value, var = pl.pallas_call(
        diffuse_first_kernel,
        out_shape=(shape(LAT * BACK, LANES), flat, flat),
        in_specs=[SMEM, VMEM],
        out_specs=[VMEM] * 3,
        scratch_shapes=buf,
        compiler_params=params(16),
        name="diffuse_first",
    )(steps, got)
    got = exchange(moved)

    block_list = pltpu.SMEM((BLOCKS + 8,), I32)
    mine = pl.pallas_call(
        lambda *refs: observe_kernel(scale, *refs),
        out_shape=flat,
        in_specs=[SMEM] + [VMEM] * 3,
        out_specs=VMEM,
        scratch_shapes=[pltpu.VMEM((COLS, 32, LANES), F32), pltpu.VMEM((2 * HI, LANES), F32), block_list],
        compiler_params=params(16),
        name="observe",
    )(counts, got, ens, slots)
    others = [lax.ppermute(mine, "member", [(i, (i + k) % 4) for i in range(4)]) for k in (1, 3, 2)]

    sent, departure = pl.pallas_call(
        lambda *refs: adjoint_kernel(scale, *refs),
        out_shape=(shape(LAT * BACK, LANES), flat),
        in_specs=[SMEM] + [VMEM] * 8,
        out_specs=[VMEM] * 2,
        scratch_shapes=[
            pltpu.VMEM((4 * LO, HI), F32),
            pltpu.VMEM((2 * HI, LANES), F32),
            pltpu.VMEM((COLS, 32, LANES), F32),
            pltpu.VMEM((COLS, GROUP * 8, LANES), F32),
            block_list,
        ],
        compiler_params=params(24),
        name="adjoint",
    )(counts, mine, *others, value, var, slots, ens)
    got = exchange(sent)

    moved = pl.pallas_call(
        diffuse_kernel,
        out_shape=shape(LAT * BACK, LANES),
        in_specs=[SMEM, VMEM],
        out_specs=VMEM,
        scratch_shapes=buf,
        compiler_params=params(16),
        name="diffuse",
    )(steps, got)
    got = exchange(moved)

    gradient = pl.pallas_call(
        gradient_kernel,
        out_shape=shape(GROUP * 8, LON),
        in_specs=[VMEM] * 2,
        out_specs=VMEM,
        compiler_params=params(16),
        name="gradient",
    )(rows, got)
    return gradient.reshape(alpha.shape), departure.reshape(1, TILES, SLOT)


def solution(mesh):
    return jax.shard_map(
        shards,
        mesh=mesh,
        in_specs=(
            P("member", None, "tile", None),
            P("member", None, None, "tile", None),
            P(),
            P("tile", None, None, None),
            P("tile", None, None, None),
            P("tile", None),
            P(None, "tile", None),
            P(None, "tile", None),
        ),
        out_specs=(P("member", None, "tile", None), P("tile", None, None)),
        check_vma=False,
    )
```

```python
import math

import jax
import jax.numpy as jnp
from jax import lax
from jax.experimental import pallas as pl
from jax.experimental.pallas import tpu as pltpu
from jax.sharding import PartitionSpec as P

FLD, LEV, ROWS, LON = 4, 4, 2, 1440
TILES, SLOT, GROUP = 32, 1024, 20
LAT = TILES * ROWS
CH = FLD * LEV
KMAX = 8

PIECES = 5
MGRP = GROUP // PIECES
HALF = LON // 2
PIECE = HALF + 2 * KMAX
LANES = 128
LINE = -(-PIECES * PIECE // LANES)
COLS = -(-LON // LANES)
OBS_ROWS = SLOT // LANES
THERE, BACK = LINE + OBS_ROWS, LINE
DEEP, WIDE = 16, 32

CHUNK = 90
CHUNKS = LON // CHUNK
HI = CH * CHUNKS
LO = 96
BLOCK = 256
BLOCKS = TILES * OBS_ROWS

F32, BF16, I32 = jnp.float32, jnp.bfloat16, jnp.int32
VMEM = pl.BlockSpec(memory_space=pltpu.VMEM)
SMEM = pl.BlockSpec(memory_space=pltpu.SMEM)


def params(mib):
    return pltpu.CompilerParams(vmem_limit_bytes=mib * 1024 * 1024)


def lanes8():
    return lax.broadcasted_iota(I32, (8, LANES), 1)


def assemble(fetch, where_from, cache):
    value, start, last = None, 0, None
    segments = []
    for lane in range(LANES):
        src = where_from(lane)
        if src is None:
            continue
        key, tile, at = src
        this = (key, tile, (lane - at) % LANES)
        if this != last:
            segments.append((lane, this))
            last = this
    for start, (key, tile, shift) in segments:
        if (key, tile, shift) not in cache:
            x = fetch(key, tile)
            cache[key, tile, shift] = pltpu.roll(x, shift, 1) if shift else x
        x = cache[key, tile, shift]
        value = x if value is None else jnp.where(lanes8() >= start, x, value)
    return value


def pack_rows(fetch, store, line):
    for mgrp in range(MGRP):
        for half in range(2):
            cache = {}
            for j in range(LINE):

                def where_from(lane):
                    piece, at = divmod(j * LANES + lane, PIECE)
                    if piece >= PIECES:
                        return None
                    col = (at - KMAX + half * HALF) % LON
                    return (piece, col // LANES, col % LANES)

                tile = assemble(lambda piece, t: fetch(piece * MGRP + mgrp, t), where_from, cache)
                store((half * MGRP * 8 + mgrp * 8) * line + j, tile)


def unpack_tile(got_ref, member, t, cache):
    piece, mgrp = divmod(member, MGRP)

    def where_from(lane):
        col = t * LANES + lane
        if col >= LON:
            return None
        half, at = divmod(col, HALF)
        at += piece * PIECE + KMAX
        return (half, at // LANES, at % LANES)

    def fetch(half, j):
        return got_ref[pl.ds((half * MGRP * 8 + mgrp * 8) * BACK + j, 8, stride=BACK), :]

    return assemble(fetch, where_from, cache)


def pack_kernel(alpha_ref, value_ref, var_ref, out_ref):
    def fetch(member, t):
        width = min(LANES, LON - t * LANES)
        tile = alpha_ref[member, :, :, t * LANES : t * LANES + width].reshape(8, width)
        if width == LANES:
            return tile
        return jnp.concatenate([tile, jnp.zeros((8, LANES - width), F32)], 1)

    def store(row, tile):
        out_ref[pl.ds(row, 8, stride=THERE), :] = tile

    pack_rows(fetch, store, THERE)
    for d in range(TILES):
        for r, ref in enumerate((value_ref, var_ref)):
            at = (d * 2 + r) * THERE + LINE
            out_ref[at : at + OBS_ROWS, :] = ref[d * OBS_ROWS : (d + 1) * OBS_ROWS, :]


def diffuse_step(src, dst):
    sub = lax.broadcasted_iota(I32, (8, LANES), 0)
    lane = lanes8()

    def plane(g):
        return [src[g, a] for a in range(DEEP)]

    above = [jnp.where(lane < WIDE, 0.0, pltpu.roll(v, WIDE, 1)) for v in plane(DEEP - 1)]
    here = plane(0)
    for g in range(DEEP):
        if g < DEEP - 1:
            below = plane(g + 1)
        else:
            below = [jnp.where(lane >= LANES - WIDE, 0.0, pltpu.roll(v, LANES - WIDE, 1)) for v in plane(0)]
        west = pltpu.roll(here[-1], 1, 0)
        west = jnp.where(sub == 0, pltpu.roll(west, 1, 1), west)
        east = pltpu.roll(here[0], 7, 0)
        east = jnp.where(sub == 7, pltpu.roll(east, LANES - 1, 1), east)
        line = [west] + here + [east]
        for a in range(DEEP):
            near = (above[a] + below[a]) + (line[a] + line[a + 2])
            dst[g, a] = 0.2 * near + (1.0 - 4.0 * 0.2) * here[a]
        above, here = here, below


def diffuse_body(steps_ref, in_ref, out_ref, one, two, turned, line):
    blocks = LANES // WIDE
    for g in range(DEEP):
        lines = []
        for q in range(blocks):
            at = (DEEP * q + g) * line
            piece = in_ref[at : at + LINE, :]
            lines += [piece, jnp.zeros((WIDE - LINE, LANES), F32)]
        turned[g] = jnp.concatenate(lines, 0).T
    for g in range(DEEP):
        for a in range(DEEP):
            one[g, a] = turned[g, pl.ds(a, 8, stride=DEEP), :]
    count = steps_ref[0]

    def pair(k, carry):
        diffuse_step(one, two)
        diffuse_step(two, one)
        return carry

    lax.fori_loop(0, lax.div(count, 2), pair, 0)

    def put(src):
        for g in range(DEEP):
            for a in range(DEEP):
                turned[g, pl.ds(a, 8, stride=DEEP), :] = src[g, a]
        for g in range(DEEP):
            lines = turned[g].T
            for q in range(blocks):
                at = (DEEP * q + g) * BACK
                out_ref[at : at + LINE, :] = lines[q * WIDE : q * WIDE + LINE]

    odd = lax.rem(count, 2)

    @pl.when(odd == 1)
    def _():
        diffuse_step(one, two)
        put(two)

    @pl.when(odd == 0)
    def _():
        put(one)


def diffuse_first_kernel(steps_ref, in_ref, out_ref, value_ref, var_ref, one, two, turned):
    diffuse_body(steps_ref, in_ref, out_ref, one, two, turned, THERE)
    for t in range(TILES):
        for r, ref in enumerate((value_ref, var_ref)):
            at = (t * 2 + r) * THERE + LINE
            ref[t * OBS_ROWS : (t + 1) * OBS_ROWS, :] = in_ref[at : at + OBS_ROWS, :]


def diffuse_kernel(steps_ref, in_ref, out_ref, one, two, turned):
    diffuse_body(steps_ref, in_ref, out_ref, one, two, turned, BACK)


def slots_kernel(count_ref, index_ref, weight_ref, out_ref, list_ref):
    def body(s, carry):
        index = index_ref[s]
        weight = weight_ref[s]
        at = index.astype(F32) + 0.5
        chan = jnp.floor(at * (1.0 / (ROWS * LON)))
        rest = at - chan * (ROWS * LON)
        below = rest > LON
        col = jnp.where(below, rest - LON, rest) - 0.5
        low, high = jnp.min(col, 0, keepdims=True), jnp.max(col, 0, keepdims=True)
        base = jnp.where(high - low > 1.5, high, low)
        chunk = jnp.floor((base + 0.5) * (1.0 / CHUNK))
        first = col == base
        rows = [chunk * CH + chan[0:1], base - chunk * CHUNK]
        for row in (jnp.logical_not(below), below):
            for column in (first, jnp.logical_not(first)):
                rows.append(jnp.sum(jnp.where(row & column, weight, 0.0), 0, keepdims=True))
        for k, row in enumerate(rows):
            for j in range(OBS_ROWS):
                out_ref[s * OBS_ROWS + j, k : k + 1, :] = row[:, j * LANES : (j + 1) * LANES]
        return carry

    lax.fori_loop(0, TILES, body, 0)
    live_blocks(count_ref, list_ref)


def live_blocks(count_ref, list_ref):
    def body(s, n):
        for j in range(OBS_ROWS):
            list_ref[n + j] = s * OBS_ROWS + j
        return n + lax.div(count_ref[s] + (LANES - 1), LANES)

    n = lax.fori_loop(0, TILES, body, 0)
    for j in range(2 * SIZES[-1]):
        list_ref[n + j] = 0
    list_ref[LISTED - 1] = n


def over_live(n, body):
    def large(i, carry):
        body(i * (2 * SIZES[0]), SIZES[0])
        return carry

    many = lax.div(n, 2 * SIZES[0])
    lax.fori_loop(0, many, large, 0)
    done = many * (2 * SIZES[0])
    left = lax.div(n - done + (2 * SIZES[-1] - 1), 2 * SIZES[-1]) * SIZES[-1]
    for size in SIZES:
        fits = left >= size

        @pl.when(fits)
        def _(done=done, size=size):
            body(done, size)

        done += jnp.where(fits, 2 * size, 0)
        left -= jnp.where(fits, size, 0)


def slot_rows(slot_ref, pair):
    blocks = [slot_ref[b] for b in pair]
    return [jnp.concatenate([x[k : k + 1] for x in blocks], 1) for k in range(6)]


def one_hot(high):
    rows = lax.broadcasted_iota(I32, (HI, BLOCK), 0).astype(F32).astype(BF16)
    return jnp.where(rows == high.astype(BF16), jnp.ones((), BF16), jnp.zeros((), BF16))


def split(x):
    high = x.astype(BF16)
    return high, (x - high.astype(F32)).astype(BF16)


SIZES = (16, 8, 4, 2)
LISTED = BLOCKS + 16


def observe_kernel(scale, list_ref, got_ref, ens_ref, slot_ref, out_ref, inc_ref, table_ref):
    for t in range(COLS):
        total = [jnp.zeros((8, LANES), F32) for f in range(FLD)]
        for m in range(GROUP):
            local = unpack_tile(got_ref, m, t, {})
            for pair in range(FLD // 2):
                ens = ens_ref[m, pair, :, t * LANES : (t + 1) * LANES].astype(F32)
                total[2 * pair] += ens[:8] * local
                total[2 * pair + 1] += ens[8:] * local
        for f in range(FLD):
            inc_ref[t, f * 8 : f * 8 + 8, :] = total[f] * scale
    for q in range(CHUNKS):
        for f in range(FLD):

            def where_from(lane):
                if lane > CHUNK:
                    return None
                col = (q * CHUNK + lane) % LON
                return (0, col // LANES, col % LANES)

            tile = assemble(lambda key, t: inc_ref[t, f * 8 : f * 8 + 8, :], where_from, {})
            table_ref[q * 32 + f * 8 : q * 32 + f * 8 + 8, :] = tile
    parts = []
    for r in range(ROWS):
        turned = table_ref[pl.ds(r, HI, stride=2), :].T
        parts.append(split(turned[:LO]))
    left = jnp.concatenate([parts[0][0], parts[1][0], parts[0][1], parts[1][1]], 0)

    out_ref[...] = jnp.zeros_like(out_ref)
    n = list_ref[LISTED - 1]
    columns = lax.broadcasted_iota(I32, (LO, BLOCK), 0).astype(F32)

    def body(start, pairs):
        for u in range(pairs):
            pair = [list_ref[start + 2 * u + h] for h in range(2)]
            high, low, w00, w01, w10, w11 = slot_rows(slot_ref, pair)
            picked = jnp.dot(left, one_hot(high), preferred_element_type=F32)
            both = picked[: 2 * LO] + picked[2 * LO :]
            here, after = columns == low, columns == low + 1.0
            value = jnp.where(here, w00, jnp.where(after, w01, 0.0)) * both[:LO]
            value += jnp.where(here, w10, jnp.where(after, w11, 0.0)) * both[LO:]
            value = jnp.sum(value, 0, keepdims=True)
            for h in range(2):
                out_ref[pl.ds(pair[h], 1), :] = value[:, h * LANES : (h + 1) * LANES]

    over_live(n, body)


def adjoint_kernel(scale, count_ref, list_ref, m0, m1, m2, m3, value_ref, var_ref, slot_ref, ens_ref, out_ref, dep_ref,
                   acc_ref, table_ref, adj_ref, proj_ref):
    slot_at = lax.broadcasted_iota(I32, (OBS_ROWS, LANES), 0) * LANES + lax.broadcasted_iota(I32, (OBS_ROWS, LANES), 1)
    for s in range(TILES):
        at = slice(s * OBS_ROWS, (s + 1) * OBS_ROWS)
        model = (m0[at, :] + m1[at, :]) + (m2[at, :] + m3[at, :])
        weighted = var_ref[at, :] * (value_ref[at, :] - model)
        dep_ref[at, :] = jnp.where(slot_at < count_ref[s], weighted, 0.0)
    acc_ref[...] = jnp.zeros_like(acc_ref)
    n = list_ref[LISTED - 1]
    columns = lax.broadcasted_iota(I32, (LO, BLOCK), 0).astype(F32).astype(BF16)

    def body(start, pairs):
        spreads, hots = [], []
        for u in range(pairs):
            at = [start + 2 * u + h for h in range(2)]
            pair = [list_ref[k] for k in at]
            high, low, w00, w01, w10, w11 = slot_rows(slot_ref, pair)
            dep = [jnp.where(k < n, dep_ref[pl.ds(b, 1), :], 0.0) for k, b in zip(at, pair)]
            dep = jnp.concatenate(dep, 1)
            here, after = columns == low.astype(BF16), columns == (low + 1.0).astype(BF16)
            halves = []
            for first, second in ((w00, w01), (w10, w11)):
                first, second = split(first * dep), split(second * dep)
                zero = jnp.zeros((), BF16)
                halves.append([jnp.where(here, x, jnp.where(after, y, zero)) for x, y in zip(first, second)])
            spreads.append(jnp.concatenate([halves[0][0], halves[1][0], halves[0][1], halves[1][1]], 0))
            hots.append(one_hot(high))
        spread, hot = jnp.concatenate(spreads, 1), jnp.concatenate(hots, 1)
        acc_ref[...] += lax.dot_general(spread, hot, (((1,), (1,)), ((), ())), preferred_element_type=F32)

    over_live(n, body)
    both = acc_ref[: 2 * LO, :] + acc_ref[2 * LO :, :]
    for r in range(ROWS):
        part = jnp.concatenate([both[r * LO : (r + 1) * LO], jnp.zeros((LANES - LO, HI), F32)], 0)
        table_ref[pl.ds(r, HI, stride=2), :] = part.T * scale
    lane = lanes8()
    for f in range(FLD):
        for t in range(COLS):
            total = jnp.zeros((8, LANES), F32)
            for q in range(-1, CHUNKS):
                first, last = max(q * CHUNK, t * LANES), min(q * CHUNK + CHUNK, t * LANES + LANES - 1, LON - 1)
                if first > last:
                    continue
                chunk = table_ref[(q % CHUNKS) * 32 + f * 8 : (q % CHUNKS) * 32 + f * 8 + 8, :]
                shift = (q * CHUNK - t * LANES) % LANES
                chunk = pltpu.roll(chunk, shift, 1) if shift else chunk
                mask = (lane >= first - t * LANES) & (lane <= last - t * LANES)
                total += jnp.where(mask, chunk, 0.0)
            adj_ref[t, f * 8 : f * 8 + 8, :] = total
    for t in range(COLS):
        adj = [adj_ref[t, f * 8 : f * 8 + 8, :] for f in range(FLD)]
        for m in range(GROUP):
            total = jnp.zeros((8, LANES), F32)
            for pair in range(FLD // 2):
                ens = ens_ref[m, pair, :, t * LANES : (t + 1) * LANES].astype(F32)
                total += ens[:8] * adj[2 * pair] + ens[8:] * adj[2 * pair + 1]
            proj_ref[t, m * 8 : m * 8 + 8, :] = total

    def store(row, tile):
        out_ref[pl.ds(row, 8, stride=BACK), :] = tile

    pack_rows(lambda m, t: proj_ref[t, m * 8 : m * 8 + 8, :], store, BACK)


def gradient_kernel(alpha_ref, got_ref, out_ref):
    for m in range(GROUP):
        cache = {}
        for t in range(COLS):
            width = min(LANES, LON - t * LANES)
            tile = unpack_tile(got_ref, m, t, cache)
            at = (m, slice(None), slice(None), slice(t * LANES, t * LANES + width))
            out_ref[at] = alpha_ref[at] - tile[:, :width].reshape(LEV, ROWS, width)


def shape(*dims, dtype=F32):
    return jax.ShapeDtypeStruct(dims, dtype)


def exchange(x):
    rows = x.shape[0] // TILES
    x = x.reshape(TILES, rows // 2, 2, LANES)
    return lax.all_to_all(x, "tile", 0, 0, tiled=True).reshape(TILES * rows, LANES)


def shards(alpha, ensemble, step_count, obs_index, obs_weight, obs_count, obs_value, inv_var):
    members = GROUP * lax.axis_size("member")
    scale = 1.0 / math.sqrt(members - 1)
    me = lax.axis_index("tile")
    steps = lax.dynamic_slice(step_count, (lax.rem(me, LEV),), (1,))
    counts = obs_count[0]
    wide = ((0, 0), (0, COLS * LANES - LON))
    ens = jnp.pad(ensemble.reshape(GROUP, 2, 16, LON), ((0, 0), (0, 0)) + wide)
    value = obs_value.reshape(TILES * OBS_ROWS, LANES)
    var = inv_var.reshape(TILES * OBS_ROWS, LANES)
    flat = shape(TILES * OBS_ROWS, LANES)

    sent = pl.pallas_call(
        pack_kernel,
        out_shape=shape(LAT * THERE, LANES),
        in_specs=[VMEM] * 3,
        out_specs=VMEM,
        compiler_params=params(16),
        name="pack",
    )(alpha, value, var)
    got = exchange(sent)

    slots, listed = pl.pallas_call(
        slots_kernel,
        out_shape=(shape(BLOCKS, 8, LANES), shape(LISTED, dtype=I32)),
        in_specs=[SMEM] + [VMEM] * 2,
        out_specs=(VMEM, SMEM),
        compiler_params=params(16),
        cost_estimate=pl.CostEstimate(flops=8000000, bytes_accessed=2097152, transcendentals=0),
        name="slots",
    )(counts, obs_index[0], obs_weight[0])

    buf = [pltpu.VMEM((DEEP, DEEP, 8, LANES), F32)] * 2 + [pltpu.VMEM((DEEP, LANES, LANES), F32)]
    moved, value, var = pl.pallas_call(
        diffuse_first_kernel,
        out_shape=(shape(LAT * BACK, LANES), flat, flat),
        in_specs=[SMEM, VMEM],
        out_specs=[VMEM] * 3,
        scratch_shapes=buf,
        compiler_params=params(16),
        name="diffuse_first",
    )(steps, got)
    got = exchange(moved)

    mine = pl.pallas_call(
        lambda *refs: observe_kernel(scale, *refs),
        out_shape=flat,
        in_specs=[SMEM] + [VMEM] * 3,
        out_specs=VMEM,
        scratch_shapes=[pltpu.VMEM((COLS, 32, LANES), F32), pltpu.VMEM((2 * HI, LANES), F32)],
        compiler_params=params(16),
        name="observe",
    )(listed, got, ens, slots)
    others = [lax.ppermute(mine, "member", [(i, (i + k) % 4) for i in range(4)]) for k in (1, 3, 2)]

    sent, departure = pl.pallas_call(
        lambda *refs: adjoint_kernel(scale, *refs),
        out_shape=(shape(LAT * BACK, LANES), flat),
        in_specs=[SMEM] * 2 + [VMEM] * 8,
        out_specs=[VMEM] * 2,
        scratch_shapes=[
            pltpu.VMEM((4 * LO, HI), F32),
            pltpu.VMEM((2 * HI, LANES), F32),
            pltpu.VMEM((COLS, 32, LANES), F32),
            pltpu.VMEM((COLS, GROUP * 8, LANES), F32),
        ],
        compiler_params=params(24),
        name="adjoint",
    )(counts, listed, mine, *others, value, var, slots, ens)
    got = exchange(sent)

    moved = pl.pallas_call(
        diffuse_kernel,
        out_shape=shape(LAT * BACK, LANES),
        in_specs=[SMEM, VMEM],
        out_specs=VMEM,
        scratch_shapes=buf,
        compiler_params=params(16),
        name="diffuse",
    )(steps, got)
    got = exchange(moved)

    gradient = pl.pallas_call(
        gradient_kernel,
        out_shape=shape(*alpha.shape),
        in_specs=[VMEM] * 2,
        out_specs=VMEM,
        compiler_params=params(16),
        name="gradient",
    )(alpha, got)
    return gradient, departure.reshape(1, TILES, SLOT)


def solution(mesh):
    return jax.shard_map(
        shards,
        mesh=mesh,
        in_specs=(
            P("member", None, "tile", None),
            P("member", None, None, "tile", None),
            P(),
            P("tile", None, None, None),
            P("tile", None, None, None),
            P("tile", None),
            P(None, "tile", None),
            P(None, "tile", None),
        ),
        out_specs=(P("member", None, "tile", None), P("tile", None, None)),
        check_vma=False,
    )
```

```python
import math

import jax
import jax.numpy as jnp
from jax import lax
from jax.experimental import pallas as pl
from jax.experimental.pallas import tpu as pltpu
from jax.sharding import PartitionSpec as P

FLD, LEV, ROWS, LON = 4, 4, 2, 1440
TILES, SLOT, GROUP = 32, 1024, 20
LAT = TILES * ROWS
CH = FLD * LEV
KMAX = 8

PIECES = 5
MGRP = GROUP // PIECES
HALF = LON // 2
PIECE = HALF + 2 * KMAX
LANES = 128
LINE = -(-PIECES * PIECE // LANES)
COLS = -(-LON // LANES)
OBS_ROWS = SLOT // LANES
HALF_VAR = OBS_ROWS // ROWS
THERE, BACK = LINE + HALF_VAR + 1, LINE
DEEP, WIDE = 16, 32

CHUNK = 90
CHUNKS = LON // CHUNK
HI = CH * CHUNKS
LO = 96
BLOCK = 256
BLOCKS = TILES * OBS_ROWS

F32, BF16, I32 = jnp.float32, jnp.bfloat16, jnp.int32
VMEM = pl.BlockSpec(memory_space=pltpu.VMEM)
SMEM = pl.BlockSpec(memory_space=pltpu.SMEM)
HBM = pl.BlockSpec(memory_space=pltpu.HBM)


def params(mib):
    return pltpu.CompilerParams(vmem_limit_bytes=mib * 1024 * 1024)


def lanes8():
    return lax.broadcasted_iota(I32, (8, LANES), 1)


def assemble(fetch, where_from, cache):
    value, start, last = None, 0, None
    segments = []
    for lane in range(LANES):
        src = where_from(lane)
        if src is None:
            continue
        key, tile, at = src
        this = (key, tile, (lane - at) % LANES)
        if this != last:
            segments.append((lane, this))
            last = this
    for start, (key, tile, shift) in segments:
        if (key, tile, shift) not in cache:
            x = fetch(key, tile)
            cache[key, tile, shift] = pltpu.roll(x, shift, 1) if shift else x
        x = cache[key, tile, shift]
        value = x if value is None else jnp.where(lanes8() >= start, x, value)
    return value


def pack_rows(fetch, store, line, halves=range(2)):
    for half in halves:
        for mgrp in range(MGRP):
            cache = {}
            for j in range(LINE):

                def where_from(lane):
                    piece, at = divmod(j * LANES + lane, PIECE)
                    if piece >= PIECES:
                        return None
                    col = (at - KMAX + half * HALF) % LON
                    return (piece, col // LANES, col % LANES)

                tile = assemble(lambda piece, t: fetch(piece * MGRP + mgrp, t), where_from, cache)
                store((half * MGRP * 8 + mgrp * 8) * line + j, tile)


def unpack_tile(got_ref, member, t, cache):
    piece, mgrp = divmod(member, MGRP)

    def where_from(lane):
        col = t * LANES + lane
        if col >= LON:
            return None
        half, at = divmod(col, HALF)
        at += piece * PIECE + KMAX
        return (half, at // LANES, at % LANES)

    def fetch(half, j):
        return got_ref[pl.ds((half * MGRP * 8 + mgrp * 8) * BACK + j, 8, stride=BACK), :]

    return assemble(fetch, where_from, cache)


def pack_kernel(member_ref, alpha_hbm, value_hbm, var_hbm, out_hbm, alpha_ref, value_ref, var_ref, out_ref, sems):
    loads = [
        pltpu.make_async_copy(src, dst, sems.at[k])
        for k, (src, dst) in enumerate(((alpha_hbm, alpha_ref), (value_hbm, value_ref), (var_hbm, var_ref)))
    ]
    for load in loads:
        load.start()

    def fetch(member, t):
        width = min(LANES, LON - t * LANES)
        tile = alpha_ref[member, :, :, t * LANES : t * LANES + width].reshape(8, width)
        if width == LANES:
            return tile
        return jnp.concatenate([tile, jnp.zeros((8, LANES - width), F32)], 1)

    def store(row, tile):
        out_ref[pl.ds(row, 8, stride=THERE), :] = tile

    loads[0].wait()
    rows = TILES * THERE
    stores = []
    for half in range(2):
        pack_rows(fetch, store, THERE, (half,))
        if half == 0:
            loads[1].wait()
            loads[2].wait()
        for d in range(half * TILES // 2, (half + 1) * TILES // 2):
            for r in range(ROWS):
                at, var_at = (d * 2 + r) * THERE + LINE, d * OBS_ROWS + r * HALF_VAR
                out_ref[at : at + HALF_VAR, :] = var_ref[var_at : var_at + HALF_VAR, :]
        for d in range(half * TILES // 2, (half + 1) * TILES // 2, 8):
            for r in range(ROWS):
                quarter = value_ref[pl.ds(d * OBS_ROWS + member_ref[0] * 2 + r, 8, stride=OBS_ROWS), :]
                out_ref[pl.ds((d * 2 + r) * THERE + THERE - 1, 8, stride=2 * THERE), :] = quarter
        at = slice(half * rows, (half + 1) * rows)
        stores.append(pltpu.make_async_copy(out_ref.at[at], out_hbm.at[at], sems.at[3 + half]))
        stores[-1].start()
    for done in stores:
        done.wait()


def diffuse_step(src, dst):
    sub = lax.broadcasted_iota(I32, (8, LANES), 0)
    lane = lanes8()

    def plane(g):
        return [src[g, a] for a in range(DEEP)]

    above = [jnp.where(lane < WIDE, 0.0, pltpu.roll(v, WIDE, 1)) for v in plane(DEEP - 1)]
    here = plane(0)
    for g in range(DEEP):
        if g < DEEP - 1:
            below = plane(g + 1)
        else:
            below = [jnp.where(lane >= LANES - WIDE, 0.0, pltpu.roll(v, LANES - WIDE, 1)) for v in plane(0)]
        west = pltpu.roll(here[-1], 1, 0)
        west = jnp.where(sub == 0, pltpu.roll(west, 1, 1), west)
        east = pltpu.roll(here[0], 7, 0)
        east = jnp.where(sub == 7, pltpu.roll(east, LANES - 1, 1), east)
        line = [west] + here + [east]
        for a in range(DEEP):
            near = (above[a] + below[a]) + (line[a] + line[a + 2])
            dst[g, a] = 0.2 * near + (1.0 - 4.0 * 0.2) * here[a]
        above, here = here, below


def diffuse_body(steps_ref, in_ref, out_ref, one, two, turned, line):
    blocks = LANES // WIDE
    for g in range(DEEP):
        lines = []
        for q in range(blocks):
            at = (DEEP * q + g) * line
            piece = in_ref[at : at + LINE, :]
            lines += [piece, jnp.zeros((WIDE - LINE, LANES), F32)]
        turned[g] = jnp.concatenate(lines, 0).T
    for g in range(DEEP):
        for a in range(DEEP):
            one[g, a] = turned[g, pl.ds(a, 8, stride=DEEP), :]
    count = steps_ref[0]

    def pair(k, carry):
        diffuse_step(one, two)
        diffuse_step(two, one)
        return carry

    lax.fori_loop(0, lax.div(count, 2), pair, 0)

    def put(src):
        for g in range(DEEP):
            for a in range(DEEP):
                turned[g, pl.ds(a, 8, stride=DEEP), :] = src[g, a]
        for g in range(DEEP):
            lines = turned[g].T
            for q in range(blocks):
                at = (DEEP * q + g) * BACK
                out_ref[at : at + LINE, :] = lines[q * WIDE : q * WIDE + LINE]

    odd = lax.rem(count, 2)

    @pl.when(odd == 1)
    def _():
        diffuse_step(one, two)
        put(two)

    @pl.when(odd == 0)
    def _():
        put(one)


def diffuse_first_kernel(steps_ref, in_ref, out_ref, value_ref, var_ref, one, two, turned):
    diffuse_body(steps_ref, in_ref, out_ref, one, two, turned, THERE)
    for row in range(LAT):
        at = row * THERE + LINE
        var_ref[row * HALF_VAR : (row + 1) * HALF_VAR, :] = in_ref[at : at + HALF_VAR, :]
    for row in range(0, LAT, 8):
        value_ref[row : row + 8, :] = in_ref[pl.ds(row * THERE + THERE - 1, 8, stride=THERE), :]


def diffuse_kernel(steps_ref, in_ref, out_ref, one, two, turned):
    diffuse_body(steps_ref, in_ref, out_ref, one, two, turned, BACK)


def slots_kernel(count_ref, index_ref, weight_ref, out_ref, list_ref):
    def body(s, carry):
        index = index_ref[s]
        weight = weight_ref[s]
        at = index.astype(F32) + 0.5
        chan = jnp.floor(at * (1.0 / (ROWS * LON)))
        rest = at - chan * (ROWS * LON)
        below = rest > LON
        col = jnp.where(below, rest - LON, rest) - 0.5
        low, high = jnp.min(col, 0, keepdims=True), jnp.max(col, 0, keepdims=True)
        base = jnp.where(high - low > 1.5, high, low)
        chunk = jnp.floor((base + 0.5) * (1.0 / CHUNK))
        first = col == base
        rows = [chunk * CH + chan[0:1], base - chunk * CHUNK]
        for row in (jnp.logical_not(below), below):
            for column in (first, jnp.logical_not(first)):
                rows.append(jnp.sum(jnp.where(row & column, weight, 0.0), 0, keepdims=True))
        for k, row in enumerate(rows):
            for j in range(OBS_ROWS):
                out_ref[s * OBS_ROWS + j, k : k + 1, :] = row[:, j * LANES : (j + 1) * LANES]
        return carry

    lax.fori_loop(0, TILES, body, 0)
    live_blocks(count_ref, list_ref)


def live_blocks(count_ref, list_ref):
    def body(s, n):
        for j in range(OBS_ROWS):
            list_ref[n + j] = s * OBS_ROWS + j
        return n + lax.div(count_ref[s] + (LANES - 1), LANES)

    n = lax.fori_loop(0, TILES, body, 0)
    for j in range(2 * SIZES[-1]):
        list_ref[n + j] = 0
    list_ref[LISTED - 1] = n


def over_live(n, body):
    def large(i, carry):
        body(i * (2 * SIZES[0]), SIZES[0])
        return carry

    many = lax.div(n, 2 * SIZES[0])
    lax.fori_loop(0, many, large, 0)
    done = many * (2 * SIZES[0])
    left = lax.div(n - done + (2 * SIZES[-1] - 1), 2 * SIZES[-1]) * SIZES[-1]
    for size in SIZES:
        fits = left >= size

        @pl.when(fits)
        def _(done=done, size=size):
            body(done, size)

        done += jnp.where(fits, 2 * size, 0)
        left -= jnp.where(fits, size, 0)


def slot_rows(slot_ref, pair):
    blocks = [slot_ref[b] for b in pair]
    return [jnp.concatenate([x[k : k + 1] for x in blocks], 1) for k in range(6)]


def one_hot(high):
    rows = lax.broadcasted_iota(I32, (HI, BLOCK), 0).astype(F32).astype(BF16)
    return jnp.where(rows == high.astype(BF16), jnp.ones((), BF16), jnp.zeros((), BF16))


def split(x):
    high = x.astype(BF16)
    return high, (x - high.astype(F32)).astype(BF16)


SIZES = (16, 8, 4, 2)
LISTED = BLOCKS + 16


def observe_kernel(scale, member_ref, list_ref, got_ref, ens_ref, slot_ref, value_ref, out_ref, inc_ref, table_ref):
    caches = [{} for m in range(GROUP)]
    for t in range(COLS):
        total = [jnp.zeros((8, LANES), F32) for f in range(FLD)]
        for m in range(GROUP):
            local = unpack_tile(got_ref, m, t, caches[m])
            for pair in range(FLD // 2):
                ens = ens_ref[m, pair, :, t * LANES : (t + 1) * LANES].astype(F32)
                total[2 * pair] += ens[:8] * local
                total[2 * pair + 1] += ens[8:] * local
        for f in range(FLD):
            inc_ref[t, f * 8 : f * 8 + 8, :] = total[f] * scale
    for q in range(CHUNKS):
        for f in range(FLD):

            def where_from(lane):
                if lane > CHUNK:
                    return None
                col = (q * CHUNK + lane) % LON
                return (0, col // LANES, col % LANES)

            tile = assemble(lambda key, t: inc_ref[t, f * 8 : f * 8 + 8, :], where_from, {})
            table_ref[q * 32 + f * 8 : q * 32 + f * 8 + 8, :] = tile
    parts = []
    for r in range(ROWS):
        turned = table_ref[pl.ds(r, HI, stride=2), :].T
        parts.append(split(turned[:LO]))
    left = jnp.concatenate([parts[0][0], parts[1][0], parts[0][1], parts[1][1]], 0)

    out_ref[...] = jnp.zeros_like(out_ref)
    n = list_ref[LISTED - 1]
    columns = lax.broadcasted_iota(I32, (LO, BLOCK), 0).astype(F32)

    def body(start, pairs):
        for u in range(pairs):
            pair = [list_ref[start + 2 * u + h] for h in range(2)]
            high, low, w00, w01, w10, w11 = slot_rows(slot_ref, pair)
            picked = jnp.dot(left, one_hot(high), preferred_element_type=F32)
            both = picked[: 2 * LO] + picked[2 * LO :]
            here, after = columns == low, columns == low + 1.0
            value = jnp.where(here, w00, jnp.where(after, w01, 0.0)) * both[:LO]
            value += jnp.where(here, w10, jnp.where(after, w11, 0.0)) * both[LO:]
            value = jnp.sum(value, 0, keepdims=True)
            for h in range(2):
                out_ref[pl.ds(pair[h], 1), :] = value[:, h * LANES : (h + 1) * LANES]

    over_live(n, body)
    for t in range(0, TILES, 8):
        for r in range(ROWS):
            at = pl.ds(t * OBS_ROWS + member_ref[0] * 2 + r, 8, stride=OBS_ROWS)
            out_ref[at, :] = out_ref[at, :] - value_ref[pl.ds(t * 2 + r, 8, stride=2), :]


def adjoint_kernel(scale, count_ref, list_ref, m0, m1, m2, m3, var_ref, slot_ref, ens_ref, out_ref, dep_ref,
                   acc_ref, table_ref, adj_ref, proj_ref):
    slot_at = lax.broadcasted_iota(I32, (OBS_ROWS, LANES), 0) * LANES + lax.broadcasted_iota(I32, (OBS_ROWS, LANES), 1)
    for s in range(TILES):
        at = slice(s * OBS_ROWS, (s + 1) * OBS_ROWS)
        excess = (m0[at, :] + m1[at, :]) + (m2[at, :] + m3[at, :])
        weighted = var_ref[at, :] * -excess
        dep_ref[at, :] = jnp.where(slot_at < count_ref[s], weighted, 0.0)
    acc_ref[...] = jnp.zeros_like(acc_ref)
    n = list_ref[LISTED - 1]
    columns = lax.broadcasted_iota(I32, (LO, BLOCK), 0).astype(F32).astype(BF16)

    def body(start, pairs):
        spreads, hots = [], []
        for u in range(pairs):
            at = [start + 2 * u + h for h in range(2)]
            pair = [list_ref[k] for k in at]
            high, low, w00, w01, w10, w11 = slot_rows(slot_ref, pair)
            dep = [jnp.where(k < n, dep_ref[pl.ds(b, 1), :], 0.0) for k, b in zip(at, pair)]
            dep = jnp.concatenate(dep, 1)
            here, after = columns == low.astype(BF16), columns == (low + 1.0).astype(BF16)
            halves = []
            for first, second in ((w00, w01), (w10, w11)):
                first, second = split(first * dep), split(second * dep)
                zero = jnp.zeros((), BF16)
                halves.append([jnp.where(here, x, jnp.where(after, y, zero)) for x, y in zip(first, second)])
            spreads.append(jnp.concatenate([halves[0][0], halves[1][0], halves[0][1], halves[1][1]], 0))
            hots.append(one_hot(high))
        spread, hot = jnp.concatenate(spreads, 1), jnp.concatenate(hots, 1)
        acc_ref[...] += lax.dot_general(spread, hot, (((1,), (1,)), ((), ())), preferred_element_type=F32)

    over_live(n, body)
    both = acc_ref[: 2 * LO, :] + acc_ref[2 * LO :, :]
    for r in range(ROWS):
        part = jnp.concatenate([both[r * LO : (r + 1) * LO], jnp.zeros((LANES - LO, HI), F32)], 0)
        table_ref[pl.ds(r, HI, stride=2), :] = part.T * scale
    lane = lanes8()
    for f in range(FLD):
        for t in range(COLS):
            total = jnp.zeros((8, LANES), F32)
            for q in range(-1, CHUNKS):
                first, last = max(q * CHUNK, t * LANES), min(q * CHUNK + CHUNK, t * LANES + LANES - 1, LON - 1)
                if first > last:
                    continue
                chunk = table_ref[(q % CHUNKS) * 32 + f * 8 : (q % CHUNKS) * 32 + f * 8 + 8, :]
                shift = (q * CHUNK - t * LANES) % LANES
                chunk = pltpu.roll(chunk, shift, 1) if shift else chunk
                mask = (lane >= first - t * LANES) & (lane <= last - t * LANES)
                total += jnp.where(mask, chunk, 0.0)
            adj_ref[t, f * 8 : f * 8 + 8, :] = total
    for t in range(COLS):
        adj = [adj_ref[t, f * 8 : f * 8 + 8, :] for f in range(FLD)]
        for m in range(GROUP):
            total = jnp.zeros((8, LANES), F32)
            for pair in range(FLD // 2):
                ens = ens_ref[m, pair, :, t * LANES : (t + 1) * LANES].astype(F32)
                total += ens[:8] * adj[2 * pair] + ens[8:] * adj[2 * pair + 1]
            proj_ref[t, m * 8 : m * 8 + 8, :] = total

    def store(row, tile):
        out_ref[pl.ds(row, 8, stride=BACK), :] = tile

    pack_rows(lambda m, t: proj_ref[t, m * 8 : m * 8 + 8, :], store, BACK)


def gradient_kernel(alpha_ref, got_ref, out_ref):
    for m in range(GROUP):
        cache = {}
        for t in range(COLS):
            width = min(LANES, LON - t * LANES)
            tile = unpack_tile(got_ref, m, t, cache)
            at = (m, slice(None), slice(None), slice(t * LANES, t * LANES + width))
            out_ref[at] = alpha_ref[at] - tile[:, :width].reshape(LEV, ROWS, width)


def shape(*dims, dtype=F32):
    return jax.ShapeDtypeStruct(dims, dtype)


def exchange(x):
    rows = x.shape[0] // TILES
    x = x.reshape(TILES, rows // 2, 2, LANES)
    return lax.all_to_all(x, "tile", 0, 0, tiled=True).reshape(TILES * rows, LANES)


def shards(alpha, ensemble, step_count, obs_index, obs_weight, obs_count, obs_value, inv_var):
    members = GROUP * lax.axis_size("member")
    scale = 1.0 / math.sqrt(members - 1)
    me = lax.axis_index("tile")
    steps = lax.dynamic_slice(step_count, (lax.rem(me, LEV),), (1,))
    counts = obs_count[0]
    member = lax.axis_index("member").reshape(1)
    wide = ((0, 0), (0, COLS * LANES - LON))
    ens = jnp.pad(ensemble.reshape(GROUP, 2, 16, LON), ((0, 0), (0, 0)) + wide)
    value = obs_value.reshape(TILES * OBS_ROWS, LANES)
    var = inv_var.reshape(TILES * OBS_ROWS, LANES)
    flat = shape(TILES * OBS_ROWS, LANES)

    sent = pl.pallas_call(
        pack_kernel,
        out_shape=shape(LAT * THERE, LANES),
        in_specs=[SMEM] + [HBM] * 3,
        out_specs=HBM,
        scratch_shapes=[
            pltpu.VMEM(alpha.shape, F32),
            pltpu.VMEM(value.shape, F32),
            pltpu.VMEM(var.shape, F32),
            pltpu.VMEM((LAT * THERE, LANES), F32),
            pltpu.SemaphoreType.DMA((5,)),
        ],
        compiler_params=params(63),
        name="pack",
    )(member, alpha, value, var)
    got = exchange(sent)

    slots, listed = pl.pallas_call(
        slots_kernel,
        out_shape=(shape(BLOCKS, 8, LANES), shape(LISTED, dtype=I32)),
        in_specs=[SMEM] + [VMEM] * 2,
        out_specs=(VMEM, SMEM),
        compiler_params=params(16),
        cost_estimate=pl.CostEstimate(flops=8000000, bytes_accessed=2097152, transcendentals=0),
        name="slots",
    )(counts, obs_index[0], obs_weight[0])

    buf = [pltpu.VMEM((DEEP, DEEP, 8, LANES), F32)] * 2 + [pltpu.VMEM((DEEP, LANES, LANES), F32)]
    moved, value, var = pl.pallas_call(
        diffuse_first_kernel,
        out_shape=(shape(LAT * BACK, LANES), shape(LAT, LANES), flat),
        in_specs=[SMEM, VMEM],
        out_specs=[VMEM] * 3,
        scratch_shapes=buf,
        compiler_params=params(16),
        name="diffuse_first",
    )(steps, got)
    got = exchange(moved)

    mine = pl.pallas_call(
        lambda *refs: observe_kernel(scale, *refs),
        out_shape=flat,
        in_specs=[SMEM] * 2 + [VMEM] * 4,
        out_specs=VMEM,
        scratch_shapes=[pltpu.VMEM((COLS, 32, LANES), F32), pltpu.VMEM((2 * HI, LANES), F32)],
        compiler_params=params(16),
        name="observe",
    )(member, listed, got, ens, slots, value)
    others = [lax.ppermute(mine, "member", [(i, (i + k) % 4) for i in range(4)]) for k in (1, 3, 2)]

    sent, departure = pl.pallas_call(
        lambda *refs: adjoint_kernel(scale, *refs),
        out_shape=(shape(LAT * BACK, LANES), flat),
        in_specs=[SMEM] * 2 + [VMEM] * 7,
        out_specs=[VMEM] * 2,
        scratch_shapes=[
            pltpu.VMEM((4 * LO, HI), F32),
            pltpu.VMEM((2 * HI, LANES), F32),
            pltpu.VMEM((COLS, 32, LANES), F32),
            pltpu.VMEM((COLS, GROUP * 8, LANES), F32),
        ],
        compiler_params=params(24),
        name="adjoint",
    )(counts, listed, mine, *others, var, slots, ens)
    got = exchange(sent)

    moved = pl.pallas_call(
        diffuse_kernel,
        out_shape=shape(LAT * BACK, LANES),
        in_specs=[SMEM, VMEM],
        out_specs=VMEM,
        scratch_shapes=buf,
        compiler_params=params(16),
        name="diffuse",
    )(steps, got)
    got = exchange(moved)

    gradient = pl.pallas_call(
        gradient_kernel,
        out_shape=shape(*alpha.shape),
        in_specs=[VMEM] * 2,
        out_specs=VMEM,
        compiler_params=params(16),
        name="gradient",
    )(alpha, got)
    return gradient, departure.reshape(1, TILES, SLOT)


def solution(mesh):
    return jax.shard_map(
        shards,
        mesh=mesh,
        in_specs=(
            P("member", None, "tile", None),
            P("member", None, None, "tile", None),
            P(),
            P("tile", None, None, None),
            P("tile", None, None, None),
            P("tile", None),
            P(None, "tile", None),
            P(None, "tile", None),
        ),
        out_specs=(P("member", None, "tile", None), P("tile", None, None)),
        check_vma=False,
    )
```

```python
import math

import jax
import jax.numpy as jnp
from jax import lax
from jax.experimental import pallas as pl
from jax.experimental.pallas import tpu as pltpu
from jax.sharding import PartitionSpec as P

FLD, LEV, ROWS, LON = 4, 4, 2, 1440
TILES, SLOT, GROUP = 32, 1024, 20
LAT = TILES * ROWS
CH = FLD * LEV
KMAX = 8

PIECES = 5
MGRP = GROUP // PIECES
HALF = LON // 2
PIECE = HALF + 2 * KMAX
LANES = 128
LINE = -(-PIECES * PIECE // LANES)
COLS = -(-LON // LANES)
OBS_ROWS = SLOT // LANES
HALF_VAR = OBS_ROWS // ROWS
THERE, BACK = LINE + HALF_VAR + 1, LINE
DEEP, WIDE = 16, 32

CHUNK = 90
CHUNKS = LON // CHUNK
HI = CH * CHUNKS
LO = 96
BLOCK = 256
BLOCKS = TILES * OBS_ROWS

F32, BF16, I32 = jnp.float32, jnp.bfloat16, jnp.int32
VMEM = pl.BlockSpec(memory_space=pltpu.VMEM)
SMEM = pl.BlockSpec(memory_space=pltpu.SMEM)
HBM = pl.BlockSpec(memory_space=pltpu.HBM)


def params(mib):
    return pltpu.CompilerParams(vmem_limit_bytes=mib * 1024 * 1024)


def lanes8():
    return lax.broadcasted_iota(I32, (8, LANES), 1)


def assemble(fetch, where_from, cache):
    value, start, last = None, 0, None
    segments = []
    for lane in range(LANES):
        src = where_from(lane)
        if src is None:
            continue
        key, tile, at = src
        this = (key, tile, (lane - at) % LANES)
        if this != last:
            segments.append((lane, this))
            last = this
    for start, (key, tile, shift) in segments:
        if (key, tile, shift) not in cache:
            x = fetch(key, tile)
            cache[key, tile, shift] = pltpu.roll(x, shift, 1) if shift else x
        x = cache[key, tile, shift]
        value = x if value is None else jnp.where(lanes8() >= start, x, value)
    return value


def pack_rows(fetch, store, line, halves=range(2)):
    for half in halves:
        for mgrp in range(MGRP):
            cache = {}
            for j in range(LINE):

                def where_from(lane):
                    piece, at = divmod(j * LANES + lane, PIECE)
                    if piece >= PIECES:
                        return None
                    col = (at - KMAX + half * HALF) % LON
                    return (piece, col // LANES, col % LANES)

                tile = assemble(lambda piece, t: fetch(piece * MGRP + mgrp, t), where_from, cache)
                store((half * MGRP * 8 + mgrp * 8) * line + j, tile)


def unpack_tile(got_ref, member, t, cache):
    piece, mgrp = divmod(member, MGRP)

    def where_from(lane):
        col = t * LANES + lane
        if col >= LON:
            return None
        half, at = divmod(col, HALF)
        at += piece * PIECE + KMAX
        return (half, at // LANES, at % LANES)

    def fetch(half, j):
        return got_ref[pl.ds((half * MGRP * 8 + mgrp * 8) * BACK + j, 8, stride=BACK), :]

    return assemble(fetch, where_from, cache)


def pack_kernel(member_ref, alpha_hbm, value_hbm, var_hbm, out_hbm, alpha_ref, value_ref, var_ref, out_ref, sems):
    loads = [
        pltpu.make_async_copy(src, dst, sems.at[k])
        for k, (src, dst) in enumerate(((alpha_hbm, alpha_ref), (value_hbm, value_ref), (var_hbm, var_ref)))
    ]
    for load in loads:
        load.start()

    def fetch(member, t):
        width = min(LANES, LON - t * LANES)
        tile = alpha_ref[member, :, :, t * LANES : t * LANES + width].reshape(8, width)
        if width == LANES:
            return tile
        return jnp.concatenate([tile, jnp.zeros((8, LANES - width), F32)], 1)

    def store(row, tile):
        out_ref[pl.ds(row, 8, stride=THERE), :] = tile

    loads[0].wait()
    rows = TILES * THERE
    stores = []
    for half in range(2):
        pack_rows(fetch, store, THERE, (half,))
        if half == 0:
            loads[1].wait()
            loads[2].wait()
        for d in range(half * TILES // 2, (half + 1) * TILES // 2):
            for r in range(ROWS):
                at, var_at = (d * 2 + r) * THERE + LINE, d * OBS_ROWS + r * HALF_VAR
                out_ref[at : at + HALF_VAR, :] = var_ref[var_at : var_at + HALF_VAR, :]
        for d in range(half * TILES // 2, (half + 1) * TILES // 2, 8):
            for r in range(ROWS):
                quarter = value_ref[pl.ds(d * OBS_ROWS + member_ref[0] * 2 + r, 8, stride=OBS_ROWS), :]
                out_ref[pl.ds((d * 2 + r) * THERE + THERE - 1, 8, stride=2 * THERE), :] = quarter
        at = slice(half * rows, (half + 1) * rows)
        stores.append(pltpu.make_async_copy(out_ref.at[at], out_hbm.at[at], sems.at[3 + half]))
        stores[-1].start()
    for done in stores:
        done.wait()


def diffuse_step(src, dst):
    sub = lax.broadcasted_iota(I32, (8, LANES), 0)
    lane = lanes8()

    def plane(g):
        return [src[g, a] for a in range(DEEP)]

    above = [jnp.where(lane < WIDE, 0.0, pltpu.roll(v, WIDE, 1)) for v in plane(DEEP - 1)]
    here = plane(0)
    for g in range(DEEP):
        if g < DEEP - 1:
            below = plane(g + 1)
        else:
            below = [jnp.where(lane >= LANES - WIDE, 0.0, pltpu.roll(v, LANES - WIDE, 1)) for v in plane(0)]
        west = pltpu.roll(here[-1], 1, 0)
        west = jnp.where(sub == 0, pltpu.roll(west, 1, 1), west)
        east = pltpu.roll(here[0], 7, 0)
        east = jnp.where(sub == 7, pltpu.roll(east, LANES - 1, 1), east)
        line = [west] + here + [east]
        for a in range(DEEP):
            near = (above[a] + below[a]) + (line[a] + line[a + 2])
            dst[g, a] = near + here[a]
        above, here = here, below


def diffuse_body(steps_ref, in_ref, out_ref, one, two, turned, line):
    blocks = LANES // WIDE
    for g in range(DEEP):
        lines = []
        for q in range(blocks):
            at = (DEEP * q + g) * line
            piece = in_ref[at : at + LINE, :]
            lines += [piece, jnp.zeros((WIDE - LINE, LANES), F32)]
        turned[g] = jnp.concatenate(lines, 0).T
    for g in range(DEEP):
        for a in range(DEEP):
            one[g, a] = turned[g, pl.ds(a, 8, stride=DEEP), :]
    count = steps_ref[0]

    def pair(k, carry):
        diffuse_step(one, two)
        diffuse_step(two, one)
        return carry

    lax.fori_loop(0, lax.div(count, 2), pair, 0)

    @pl.when(lax.rem(count, 2) == 1)
    def _():
        diffuse_step(one, two)
        one[...] = two[...]

    factor = lax.fori_loop(0, count, lambda k, x: x * 0.2, jnp.float32(1.0))
    for g in range(DEEP):
        for a in range(DEEP):
            turned[g, pl.ds(a, 8, stride=DEEP), :] = one[g, a] * factor
    for g in range(DEEP):
        lines = turned[g].T
        for q in range(blocks):
            at = (DEEP * q + g) * BACK
            out_ref[at : at + LINE, :] = lines[q * WIDE : q * WIDE + LINE]


def diffuse_first_kernel(steps_ref, in_ref, out_ref, value_ref, var_ref, one, two, turned):
    diffuse_body(steps_ref, in_ref, out_ref, one, two, turned, THERE)
    for row in range(LAT):
        at = row * THERE + LINE
        var_ref[row * HALF_VAR : (row + 1) * HALF_VAR, :] = in_ref[at : at + HALF_VAR, :]
    for row in range(0, LAT, 8):
        value_ref[row : row + 8, :] = in_ref[pl.ds(row * THERE + THERE - 1, 8, stride=THERE), :]


def diffuse_kernel(steps_ref, in_ref, out_ref, one, two, turned):
    diffuse_body(steps_ref, in_ref, out_ref, one, two, turned, BACK)


def slots_kernel(count_ref, index_ref, weight_ref, out_ref, list_ref):
    def body(s, carry):
        index = index_ref[s]
        weight = weight_ref[s]
        at = index.astype(F32) + 0.5
        chan = jnp.floor(at * (1.0 / (ROWS * LON)))
        rest = at - chan * (ROWS * LON)
        below = rest > LON
        col = jnp.where(below, rest - LON, rest) - 0.5
        low, high = jnp.min(col, 0, keepdims=True), jnp.max(col, 0, keepdims=True)
        base = jnp.where(high - low > 1.5, high, low)
        chunk = jnp.floor((base + 0.5) * (1.0 / CHUNK))
        first = col == base
        rows = [chunk * CH + chan[0:1], base - chunk * CHUNK]
        for row in (jnp.logical_not(below), below):
            for column in (first, jnp.logical_not(first)):
                rows.append(jnp.sum(jnp.where(row & column, weight, 0.0), 0, keepdims=True))
        for k, row in enumerate(rows):
            for j in range(OBS_ROWS):
                out_ref[s * OBS_ROWS + j, k : k + 1, :] = row[:, j * LANES : (j + 1) * LANES]
        return carry

    lax.fori_loop(0, TILES, body, 0)
    live_blocks(count_ref, list_ref)


def live_blocks(count_ref, list_ref):
    def body(s, n):
        for j in range(OBS_ROWS):
            list_ref[n + j] = s * OBS_ROWS + j
        return n + lax.div(count_ref[s] + (LANES - 1), LANES)

    n = lax.fori_loop(0, TILES, body, 0)
    for j in range(2 * SIZES[-1]):
        list_ref[n + j] = 0
    list_ref[LISTED - 1] = n


def over_live(n, body):
    def large(i, carry):
        body(i * (2 * SIZES[0]), SIZES[0])
        return carry

    many = lax.div(n, 2 * SIZES[0])
    lax.fori_loop(0, many, large, 0)
    done = many * (2 * SIZES[0])
    left = lax.div(n - done + (2 * SIZES[-1] - 1), 2 * SIZES[-1]) * SIZES[-1]
    for size in SIZES:
        fits = left >= size

        @pl.when(fits)
        def _(done=done, size=size):
            body(done, size)

        done += jnp.where(fits, 2 * size, 0)
        left -= jnp.where(fits, size, 0)


def slot_rows(slot_ref, pair):
    blocks = [slot_ref[b] for b in pair]
    return [jnp.concatenate([x[k : k + 1] for x in blocks], 1) for k in range(6)]


def one_hot(high):
    rows = lax.broadcasted_iota(I32, (HI, BLOCK), 0).astype(F32).astype(BF16)
    return jnp.where(rows == high.astype(BF16), jnp.ones((), BF16), jnp.zeros((), BF16))


def split(x):
    high = x.astype(BF16)
    return high, (x - high.astype(F32)).astype(BF16)


SIZES = (16, 8, 4, 2)
LISTED = BLOCKS + 16


def observe_kernel(scale, member_ref, list_ref, got_ref, ens_ref, slot_ref, value_ref, out_ref, inc_ref, table_ref):
    caches = [{} for m in range(GROUP)]
    for t in range(COLS):
        total = [jnp.zeros((8, LANES), F32) for f in range(FLD)]
        for m in range(GROUP):
            local = unpack_tile(got_ref, m, t, caches[m])
            for pair in range(FLD // 2):
                ens = ens_ref[m, pair, :, t * LANES : (t + 1) * LANES].astype(F32)
                total[2 * pair] += ens[:8] * local
                total[2 * pair + 1] += ens[8:] * local
        for f in range(FLD):
            inc_ref[t, f * 8 : f * 8 + 8, :] = total[f] * scale
    for q in range(CHUNKS):
        for f in range(FLD):

            def where_from(lane):
                if lane > CHUNK:
                    return None
                col = (q * CHUNK + lane) % LON
                return (0, col // LANES, col % LANES)

            tile = assemble(lambda key, t: inc_ref[t, f * 8 : f * 8 + 8, :], where_from, {})
            table_ref[q * 32 + f * 8 : q * 32 + f * 8 + 8, :] = tile
    parts = []
    for r in range(ROWS):
        turned = table_ref[pl.ds(r, HI, stride=2), :].T
        parts.append(split(turned[:LO]))
    left = jnp.concatenate([parts[0][0], parts[1][0], parts[0][1], parts[1][1]], 0)

    out_ref[...] = jnp.zeros_like(out_ref)
    n = list_ref[LISTED - 1]
    columns = lax.broadcasted_iota(I32, (LO, BLOCK), 0).astype(F32)

    def body(start, pairs):
        for u in range(pairs):
            pair = [list_ref[start + 2 * u + h] for h in range(2)]
            high, low, w00, w01, w10, w11 = slot_rows(slot_ref, pair)
            picked = jnp.dot(left, one_hot(high), preferred_element_type=F32)
            both = picked[: 2 * LO] + picked[2 * LO :]
            here, after = columns == low, columns == low + 1.0
            value = jnp.where(here, w00, jnp.where(after, w01, 0.0)) * both[:LO]
            value += jnp.where(here, w10, jnp.where(after, w11, 0.0)) * both[LO:]
            value = jnp.sum(value, 0, keepdims=True)
            for h in range(2):
                out_ref[pl.ds(pair[h], 1), :] = value[:, h * LANES : (h + 1) * LANES]

    over_live(n, body)
    for t in range(0, TILES, 8):
        for r in range(ROWS):
            at = pl.ds(t * OBS_ROWS + member_ref[0] * 2 + r, 8, stride=OBS_ROWS)
            out_ref[at, :] = out_ref[at, :] - value_ref[pl.ds(t * 2 + r, 8, stride=2), :]


def adjoint_kernel(scale, count_ref, list_ref, m0, m1, m2, m3, var_ref, slot_ref, ens_ref, out_ref, dep_ref,
                   acc_ref, table_ref, adj_ref, proj_ref):
    slot_at = lax.broadcasted_iota(I32, (OBS_ROWS, LANES), 0) * LANES + lax.broadcasted_iota(I32, (OBS_ROWS, LANES), 1)
    for s in range(TILES):
        at = slice(s * OBS_ROWS, (s + 1) * OBS_ROWS)
        excess = (m0[at, :] + m1[at, :]) + (m2[at, :] + m3[at, :])
        weighted = var_ref[at, :] * -excess
        dep_ref[at, :] = jnp.where(slot_at < count_ref[s], weighted, 0.0)
    acc_ref[...] = jnp.zeros_like(acc_ref)
    n = list_ref[LISTED - 1]
    columns = lax.broadcasted_iota(I32, (LO, BLOCK), 0).astype(F32).astype(BF16)

    def body(start, pairs):
        spreads, hots = [], []
        for u in range(pairs):
            at = [start + 2 * u + h for h in range(2)]
            pair = [list_ref[k] for k in at]
            high, low, w00, w01, w10, w11 = slot_rows(slot_ref, pair)
            dep = [jnp.where(k < n, dep_ref[pl.ds(b, 1), :], 0.0) for k, b in zip(at, pair)]
            dep = jnp.concatenate(dep, 1)
            here, after = columns == low.astype(BF16), columns == (low + 1.0).astype(BF16)
            halves = []
            for first, second in ((w00, w01), (w10, w11)):
                first, second = split(first * dep), split(second * dep)
                zero = jnp.zeros((), BF16)
                halves.append([jnp.where(here, x, jnp.where(after, y, zero)) for x, y in zip(first, second)])
            spreads.append(jnp.concatenate([halves[0][0], halves[1][0], halves[0][1], halves[1][1]], 0))
            hots.append(one_hot(high))
        spread, hot = jnp.concatenate(spreads, 1), jnp.concatenate(hots, 1)
        acc_ref[...] += lax.dot_general(spread, hot, (((1,), (1,)), ((), ())), preferred_element_type=F32)

    over_live(n, body)
    both = acc_ref[: 2 * LO, :] + acc_ref[2 * LO :, :]
    for r in range(ROWS):
        part = jnp.concatenate([both[r * LO : (r + 1) * LO], jnp.zeros((LANES - LO, HI), F32)], 0)
        table_ref[pl.ds(r, HI, stride=2), :] = part.T * scale
    lane = lanes8()
    for f in range(FLD):
        for t in range(COLS):
            total = jnp.zeros((8, LANES), F32)
            for q in range(-1, CHUNKS):
                first, last = max(q * CHUNK, t * LANES), min(q * CHUNK + CHUNK, t * LANES + LANES - 1, LON - 1)
                if first > last:
                    continue
                chunk = table_ref[(q % CHUNKS) * 32 + f * 8 : (q % CHUNKS) * 32 + f * 8 + 8, :]
                shift = (q * CHUNK - t * LANES) % LANES
                chunk = pltpu.roll(chunk, shift, 1) if shift else chunk
                mask = (lane >= first - t * LANES) & (lane <= last - t * LANES)
                total += jnp.where(mask, chunk, 0.0)
            adj_ref[t, f * 8 : f * 8 + 8, :] = total
    for t in range(COLS):
        adj = [adj_ref[t, f * 8 : f * 8 + 8, :] for f in range(FLD)]
        for m in range(GROUP):
            total = jnp.zeros((8, LANES), F32)
            for pair in range(FLD // 2):
                ens = ens_ref[m, pair, :, t * LANES : (t + 1) * LANES].astype(F32)
                total += ens[:8] * adj[2 * pair] + ens[8:] * adj[2 * pair + 1]
            proj_ref[t, m * 8 : m * 8 + 8, :] = total

    def store(row, tile):
        out_ref[pl.ds(row, 8, stride=BACK), :] = tile

    pack_rows(lambda m, t: proj_ref[t, m * 8 : m * 8 + 8, :], store, BACK)


def gradient_kernel(alpha_ref, got_ref, out_hbm, out_ref, sems):
    stores = []
    for m in range(GROUP):
        cache = {}
        for t in range(COLS):
            width = min(LANES, LON - t * LANES)
            tile = unpack_tile(got_ref, m, t, cache)
            at = (m, slice(None), slice(None), slice(t * LANES, t * LANES + width))
            out_ref[at] = alpha_ref[at] - tile[:, :width].reshape(LEV, ROWS, width)
        if m % MGRP == MGRP - 1:
            at = slice(m + 1 - MGRP, m + 1)
            stores.append(pltpu.make_async_copy(out_ref.at[at], out_hbm.at[at], sems.at[len(stores)]))
            stores[-1].start()
    for done in stores:
        done.wait()


def shape(*dims, dtype=F32):
    return jax.ShapeDtypeStruct(dims, dtype)


def exchange(x):
    rows = x.shape[0] // TILES
    x = x.reshape(TILES, rows // 2, 2, LANES)
    return lax.all_to_all(x, "tile", 0, 0, tiled=True).reshape(TILES * rows, LANES)


def shards(alpha, ensemble, step_count, obs_index, obs_weight, obs_count, obs_value, inv_var):
    members = GROUP * lax.axis_size("member")
    scale = 1.0 / math.sqrt(members - 1)
    me = lax.axis_index("tile")
    steps = lax.dynamic_slice(step_count, (lax.rem(me, LEV),), (1,))
    counts = obs_count[0]
    member = lax.axis_index("member").reshape(1)
    wide = ((0, 0), (0, COLS * LANES - LON))
    ens = jnp.pad(ensemble.reshape(GROUP, 2, 16, LON), ((0, 0), (0, 0)) + wide)
    value = obs_value.reshape(TILES * OBS_ROWS, LANES)
    var = inv_var.reshape(TILES * OBS_ROWS, LANES)
    flat = shape(TILES * OBS_ROWS, LANES)

    sent = pl.pallas_call(
        pack_kernel,
        out_shape=shape(LAT * THERE, LANES),
        in_specs=[SMEM] + [HBM] * 3,
        out_specs=HBM,
        scratch_shapes=[
            pltpu.VMEM(alpha.shape, F32),
            pltpu.VMEM(value.shape, F32),
            pltpu.VMEM(var.shape, F32),
            pltpu.VMEM((LAT * THERE, LANES), F32),
            pltpu.SemaphoreType.DMA((5,)),
        ],
        compiler_params=params(63),
        name="pack",
    )(member, alpha, value, var)
    got = exchange(sent)

    slots, listed = pl.pallas_call(
        slots_kernel,
        out_shape=(shape(BLOCKS, 8, LANES), shape(LISTED, dtype=I32)),
        in_specs=[SMEM] + [VMEM] * 2,
        out_specs=(VMEM, SMEM),
        compiler_params=params(16),
        cost_estimate=pl.CostEstimate(flops=8000000, bytes_accessed=2097152, transcendentals=0),
        name="slots",
    )(counts, obs_index[0], obs_weight[0])

    buf = [pltpu.VMEM((DEEP, DEEP, 8, LANES), F32)] * 2 + [pltpu.VMEM((DEEP, LANES, LANES), F32)]
    moved, value, var = pl.pallas_call(
        diffuse_first_kernel,
        out_shape=(shape(LAT * BACK, LANES), shape(LAT, LANES), flat),
        in_specs=[SMEM, VMEM],
        out_specs=[VMEM] * 3,
        scratch_shapes=buf,
        compiler_params=params(16),
        name="diffuse_first",
    )(steps, got)
    got = exchange(moved)

    mine = pl.pallas_call(
        lambda *refs: observe_kernel(scale, *refs),
        out_shape=flat,
        in_specs=[SMEM] * 2 + [VMEM] * 4,
        out_specs=VMEM,
        scratch_shapes=[pltpu.VMEM((COLS, 32, LANES), F32), pltpu.VMEM((2 * HI, LANES), F32)],
        compiler_params=params(16),
        name="observe",
    )(member, listed, got, ens, slots, value)
    others = [lax.ppermute(mine, "member", [(i, (i + k) % 4) for i in range(4)]) for k in (1, 3, 2)]

    sent, departure = pl.pallas_call(
        lambda *refs: adjoint_kernel(scale, *refs),
        out_shape=(shape(LAT * BACK, LANES), flat),
        in_specs=[SMEM] * 2 + [VMEM] * 7,
        out_specs=[VMEM] * 2,
        scratch_shapes=[
            pltpu.VMEM((4 * LO, HI), F32),
            pltpu.VMEM((2 * HI, LANES), F32),
            pltpu.VMEM((COLS, 32, LANES), F32),
            pltpu.VMEM((COLS, GROUP * 8, LANES), F32),
        ],
        compiler_params=params(24),
        name="adjoint",
    )(counts, listed, mine, *others, var, slots, ens)
    got = exchange(sent)

    moved = pl.pallas_call(
        diffuse_kernel,
        out_shape=shape(LAT * BACK, LANES),
        in_specs=[SMEM, VMEM],
        out_specs=VMEM,
        scratch_shapes=buf,
        compiler_params=params(16),
        name="diffuse",
    )(steps, got)
    got = exchange(moved)

    gradient = pl.pallas_call(
        gradient_kernel,
        out_shape=shape(*alpha.shape),
        in_specs=[VMEM] * 2,
        out_specs=HBM,
        scratch_shapes=[pltpu.VMEM(alpha.shape, F32), pltpu.SemaphoreType.DMA((PIECES,))],
        compiler_params=params(16),
        name="gradient",
    )(alpha, got)
    return gradient, departure.reshape(1, TILES, SLOT)


def solution(mesh):
    return jax.shard_map(
        shards,
        mesh=mesh,
        in_specs=(
            P("member", None, "tile", None),
            P("member", None, None, "tile", None),
            P(),
            P("tile", None, None, None),
            P("tile", None, None, None),
            P("tile", None),
            P(None, "tile", None),
            P(None, "tile", None),
        ),
        out_specs=(P("member", None, "tile", None), P("tile", None, None)),
        check_vma=False,
    )
```

```python
import math

import jax
import jax.numpy as jnp
from jax import lax
from jax.experimental import pallas as pl
from jax.experimental.pallas import tpu as pltpu
from jax.sharding import PartitionSpec as P

FLD, LEV, ROWS, LON = 4, 4, 2, 1440
TILES, SLOT, GROUP = 32, 1024, 20
LAT = TILES * ROWS
CH = FLD * LEV
KMAX = 8

PIECES = 5
MGRP = GROUP // PIECES
HALF = LON // 2
PIECE = HALF + 2 * KMAX
LANES = 128
LINE = -(-PIECES * PIECE // LANES)
COLS = -(-LON // LANES)
OBS_ROWS = SLOT // LANES
HALF_VAR = OBS_ROWS // ROWS
THERE, BACK = LINE + HALF_VAR + 1, LINE
DEEP, WIDE = 16, 32

CHUNK = 90
CHUNKS = LON // CHUNK
HI = CH * CHUNKS
LO = 96
BLOCK = 256
BLOCKS = TILES * OBS_ROWS

F32, BF16, I32 = jnp.float32, jnp.bfloat16, jnp.int32
VMEM = pl.BlockSpec(memory_space=pltpu.VMEM)
SMEM = pl.BlockSpec(memory_space=pltpu.SMEM)
HBM = pl.BlockSpec(memory_space=pltpu.HBM)


def params(mib):
    return pltpu.CompilerParams(vmem_limit_bytes=mib * 1024 * 1024)


def lanes8():
    return lax.broadcasted_iota(I32, (8, LANES), 1)


def assemble(fetch, where_from, cache):
    value, start, last = None, 0, None
    segments = []
    for lane in range(LANES):
        src = where_from(lane)
        if src is None:
            continue
        key, tile, at = src
        this = (key, tile, (lane - at) % LANES)
        if this != last:
            segments.append((lane, this))
            last = this
    for start, (key, tile, shift) in segments:
        if (key, tile, shift) not in cache:
            x = fetch(key, tile)
            cache[key, tile, shift] = pltpu.roll(x, shift, 1) if shift else x
        x = cache[key, tile, shift]
        value = x if value is None else jnp.where(lanes8() >= start, x, value)
    return value


def pack_rows(fetch, store, line, halves=range(2)):
    for half in halves:
        for mgrp in range(MGRP):
            cache = {}
            for j in range(LINE):

                def where_from(lane):
                    piece, at = divmod(j * LANES + lane, PIECE)
                    if piece >= PIECES:
                        return None
                    col = (at - KMAX + half * HALF) % LON
                    return (piece, col // LANES, col % LANES)

                tile = assemble(lambda piece, t: fetch(piece * MGRP + mgrp, t), where_from, cache)
                store((half * MGRP * 8 + mgrp * 8) * line + j, tile)


def unpack_tile(got_ref, member, t, cache):
    piece, mgrp = divmod(member, MGRP)

    def where_from(lane):
        col = t * LANES + lane
        if col >= LON:
            return None
        half, at = divmod(col, HALF)
        at += piece * PIECE + KMAX
        return (half, at // LANES, at % LANES)

    def fetch(half, j):
        return got_ref[pl.ds((half * MGRP * 8 + mgrp * 8) * BACK + j, 8, stride=BACK), :]

    return assemble(fetch, where_from, cache)


def pack_kernel(member_ref, alpha_hbm, value_hbm, var_hbm, out_hbm, alpha_ref, value_ref, var_ref, out_ref, sems):
    loads = [
        pltpu.make_async_copy(src, dst, sems.at[k])
        for k, (src, dst) in enumerate(((alpha_hbm, alpha_ref), (value_hbm, value_ref), (var_hbm, var_ref)))
    ]
    for load in loads:
        load.start()

    def fetch(member, t):
        width = min(LANES, LON - t * LANES)
        tile = alpha_ref[member, :, :, t * LANES : t * LANES + width].reshape(8, width)
        if width == LANES:
            return tile
        return jnp.concatenate([tile, jnp.zeros((8, LANES - width), F32)], 1)

    def store(row, tile):
        out_ref[pl.ds(row, 8, stride=THERE), :] = tile

    loads[0].wait()
    rows = TILES * THERE
    stores = []
    for half in range(2):
        pack_rows(fetch, store, THERE, (half,))
        if half == 0:
            loads[1].wait()
            loads[2].wait()
        for d in range(half * TILES // 2, (half + 1) * TILES // 2):
            for r in range(ROWS):
                at, var_at = (d * 2 + r) * THERE + LINE, d * OBS_ROWS + r * HALF_VAR
                out_ref[at : at + HALF_VAR, :] = var_ref[var_at : var_at + HALF_VAR, :]
        for d in range(half * TILES // 2, (half + 1) * TILES // 2, 8):
            for r in range(ROWS):
                quarter = value_ref[pl.ds(d * OBS_ROWS + member_ref[0] * 2 + r, 8, stride=OBS_ROWS), :]
                out_ref[pl.ds((d * 2 + r) * THERE + THERE - 1, 8, stride=2 * THERE), :] = quarter
        at = slice(half * rows, (half + 1) * rows)
        stores.append(pltpu.make_async_copy(out_ref.at[at], out_hbm.at[at], sems.at[3 + half]))
        stores[-1].start()
    for done in stores:
        done.wait()


def diffuse_step(src, dst):
    sub = lax.broadcasted_iota(I32, (8, LANES), 0)
    lane = lanes8()

    def plane(g):
        return [src[g, a] for a in range(DEEP)]

    above = [jnp.where(lane < WIDE, 0.0, pltpu.roll(v, WIDE, 1)) for v in plane(DEEP - 1)]
    here = plane(0)
    for g in range(DEEP):
        if g < DEEP - 1:
            below = plane(g + 1)
        else:
            below = [jnp.where(lane >= LANES - WIDE, 0.0, pltpu.roll(v, LANES - WIDE, 1)) for v in plane(0)]
        west = pltpu.roll(here[-1], 1, 0)
        west = jnp.where(sub == 0, pltpu.roll(west, 1, 1), west)
        east = pltpu.roll(here[0], 7, 0)
        east = jnp.where(sub == 7, pltpu.roll(east, LANES - 1, 1), east)
        line = [west] + here + [east]
        for a in range(DEEP):
            near = (above[a] + below[a]) + (line[a] + line[a + 2])
            dst[g, a] = near + here[a]
        above, here = here, below


def diffuse_body(steps_ref, in_ref, out_ref, one, two, turned, line):
    blocks = LANES // WIDE
    for g in range(DEEP):
        lines = []
        for q in range(blocks):
            at = (DEEP * q + g) * line
            piece = in_ref[at : at + LINE, :]
            lines += [piece, jnp.zeros((WIDE - LINE, LANES), F32)]
        turned[g] = jnp.concatenate(lines, 0).T
    for g in range(DEEP):
        for a in range(DEEP):
            one[g, a] = turned[g, pl.ds(a, 8, stride=DEEP), :]
    count = steps_ref[0]

    def pair(k, carry):
        diffuse_step(one, two)
        diffuse_step(two, one)
        return carry

    lax.fori_loop(0, lax.div(count, 2), pair, 0)

    @pl.when(lax.rem(count, 2) == 1)
    def _():
        diffuse_step(one, two)
        one[...] = two[...]

    factor = lax.fori_loop(0, count, lambda k, x: x * 0.2, jnp.float32(1.0))
    for g in range(DEEP):
        for a in range(DEEP):
            turned[g, pl.ds(a, 8, stride=DEEP), :] = one[g, a] * factor
    for g in range(DEEP):
        lines = turned[g].T
        for q in range(blocks):
            at = (DEEP * q + g) * BACK
            out_ref[at : at + LINE, :] = lines[q * WIDE : q * WIDE + LINE]


def diffuse_first_kernel(steps_ref, in_ref, out_ref, value_ref, var_ref, one, two, turned):
    diffuse_body(steps_ref, in_ref, out_ref, one, two, turned, THERE)
    for row in range(LAT):
        at = row * THERE + LINE
        var_ref[row * HALF_VAR : (row + 1) * HALF_VAR, :] = in_ref[at : at + HALF_VAR, :]
    for row in range(0, LAT, 8):
        value_ref[row : row + 8, :] = in_ref[pl.ds(row * THERE + THERE - 1, 8, stride=THERE), :]


def diffuse_kernel(steps_ref, in_ref, out_ref, one, two, turned):
    diffuse_body(steps_ref, in_ref, out_ref, one, two, turned, BACK)


def slots_kernel(count_ref, index_ref, weight_ref, out_ref, list_ref):
    def body(s, carry):
        index = index_ref[s]
        weight = weight_ref[s]
        at = index.astype(F32) + 0.5
        chan = jnp.floor(at * (1.0 / (ROWS * LON)))
        rest = at - chan * (ROWS * LON)
        below = rest > LON
        col = jnp.where(below, rest - LON, rest) - 0.5
        low, high = jnp.min(col, 0, keepdims=True), jnp.max(col, 0, keepdims=True)
        base = jnp.where(high - low > 1.5, high, low)
        chunk = jnp.floor((base + 0.5) * (1.0 / CHUNK))
        first = col == base
        rows = [chunk * CH + chan[0:1], base - chunk * CHUNK]
        for row in (jnp.logical_not(below), below):
            for column in (first, jnp.logical_not(first)):
                rows.append(jnp.sum(jnp.where(row & column, weight, 0.0), 0, keepdims=True))
        for k, row in enumerate(rows):
            for j in range(OBS_ROWS):
                out_ref[s * OBS_ROWS + j, k : k + 1, :] = row[:, j * LANES : (j + 1) * LANES]
        return carry

    lax.fori_loop(0, TILES, body, 0)
    live_blocks(count_ref, list_ref)


def live_blocks(count_ref, list_ref):
    def body(s, n):
        for j in range(OBS_ROWS):
            list_ref[n + j] = s * OBS_ROWS + j
        return n + lax.div(count_ref[s] + (LANES - 1), LANES)

    n = lax.fori_loop(0, TILES, body, 0)
    for j in range(2 * SIZES[-1]):
        list_ref[n + j] = 0
    list_ref[LISTED - 1] = n


def over_live(n, body):
    def large(i, carry):
        body(i * (2 * SIZES[0]), SIZES[0])
        return carry

    many = lax.div(n, 2 * SIZES[0])
    lax.fori_loop(0, many, large, 0)
    done = many * (2 * SIZES[0])
    left = lax.div(n - done + (2 * SIZES[-1] - 1), 2 * SIZES[-1]) * SIZES[-1]
    for size in SIZES:
        fits = left >= size

        @pl.when(fits)
        def _(done=done, size=size):
            body(done, size)

        done += jnp.where(fits, 2 * size, 0)
        left -= jnp.where(fits, size, 0)


def slot_rows(slot_ref, pair):
    blocks = [slot_ref[b] for b in pair]
    return [jnp.concatenate([x[k : k + 1] for x in blocks], 1) for k in range(6)]


def one_hot(high):
    rows = lax.broadcasted_iota(I32, (HI, BLOCK), 0).astype(F32).astype(BF16)
    return jnp.where(rows == high.astype(BF16), jnp.ones((), BF16), jnp.zeros((), BF16))


def split(x):
    high = x.astype(BF16)
    return high, (x - high.astype(F32)).astype(BF16)


SIZES = (32, 16, 8, 4, 2)
LISTED = BLOCKS + 16


def observe_kernel(scale, member_ref, list_ref, got_ref, ens_ref, slot_ref, value_ref, out_ref, inc_ref, table_ref):
    caches = [{} for m in range(GROUP)]
    for t in range(COLS):
        total = [jnp.zeros((8, LANES), F32) for f in range(FLD)]
        for m in range(GROUP):
            local = unpack_tile(got_ref, m, t, caches[m])
            for pair in range(FLD // 2):
                ens = ens_ref[m, pair, :, t * LANES : (t + 1) * LANES].astype(F32)
                total[2 * pair] += ens[:8] * local
                total[2 * pair + 1] += ens[8:] * local
        for f in range(FLD):
            inc_ref[t, f * 8 : f * 8 + 8, :] = total[f] * scale
    for q in range(CHUNKS):
        for f in range(FLD):

            def where_from(lane):
                if lane > CHUNK:
                    return None
                col = (q * CHUNK + lane) % LON
                return (0, col // LANES, col % LANES)

            tile = assemble(lambda key, t: inc_ref[t, f * 8 : f * 8 + 8, :], where_from, {})
            table_ref[q * 32 + f * 8 : q * 32 + f * 8 + 8, :] = tile
    parts = []
    for r in range(ROWS):
        turned = table_ref[pl.ds(r, HI, stride=2), :].T
        parts.append(split(turned[:LO]))
    left = jnp.concatenate([parts[0][0], parts[1][0], parts[0][1], parts[1][1]], 0)

    out_ref[...] = jnp.zeros_like(out_ref)
    n = list_ref[LISTED - 1]
    columns = lax.broadcasted_iota(I32, (LO, BLOCK), 0).astype(F32)

    def body(start, pairs):
        for u in range(pairs):
            pair = [list_ref[start + 2 * u + h] for h in range(2)]
            high, low, w00, w01, w10, w11 = slot_rows(slot_ref, pair)
            picked = jnp.dot(left, one_hot(high), preferred_element_type=F32)
            both = picked[: 2 * LO] + picked[2 * LO :]
            here, after = columns == low, columns == low + 1.0
            value = jnp.where(here, w00, jnp.where(after, w01, 0.0)) * both[:LO]
            value += jnp.where(here, w10, jnp.where(after, w11, 0.0)) * both[LO:]
            value = jnp.sum(value, 0, keepdims=True)
            for h in range(2):
                out_ref[pl.ds(pair[h], 1), :] = value[:, h * LANES : (h + 1) * LANES]

    over_live(n, body)
    for t in range(0, TILES, 8):
        for r in range(ROWS):
            at = pl.ds(t * OBS_ROWS + member_ref[0] * 2 + r, 8, stride=OBS_ROWS)
            out_ref[at, :] = out_ref[at, :] - value_ref[pl.ds(t * 2 + r, 8, stride=2), :]


def adjoint_kernel(scale, count_ref, list_ref, m0, m1, m2, m3, var_ref, slot_ref, ens_ref, out_ref, dep_ref,
                   acc_ref, table_ref, adj_ref, proj_ref):
    slot_at = lax.broadcasted_iota(I32, (OBS_ROWS, LANES), 0) * LANES + lax.broadcasted_iota(I32, (OBS_ROWS, LANES), 1)
    for s in range(TILES):
        at = slice(s * OBS_ROWS, (s + 1) * OBS_ROWS)
        excess = (m0[at, :] + m1[at, :]) + (m2[at, :] + m3[at, :])
        weighted = var_ref[at, :] * -excess
        dep_ref[at, :] = jnp.where(slot_at < count_ref[s], weighted, 0.0)
    acc_ref[...] = jnp.zeros_like(acc_ref)
    n = list_ref[LISTED - 1]
    columns = lax.broadcasted_iota(I32, (LO, BLOCK), 0).astype(F32).astype(BF16)

    def body(start, pairs):
        spreads, hots = [], []
        for u in range(pairs):
            at = [start + 2 * u + h for h in range(2)]
            pair = [list_ref[k] for k in at]
            high, low, w00, w01, w10, w11 = slot_rows(slot_ref, pair)
            dep = [jnp.where(k < n, dep_ref[pl.ds(b, 1), :], 0.0) for k, b in zip(at, pair)]
            dep = jnp.concatenate(dep, 1)
            here, after = columns == low.astype(BF16), columns == (low + 1.0).astype(BF16)
            halves = []
            for first, second in ((w00, w01), (w10, w11)):
                first, second = split(first * dep), split(second * dep)
                zero = jnp.zeros((), BF16)
                halves.append([jnp.where(here, x, jnp.where(after, y, zero)) for x, y in zip(first, second)])
            spreads.append(jnp.concatenate([halves[0][0], halves[1][0], halves[0][1], halves[1][1]], 0))
            hots.append(one_hot(high))
        spread, hot = jnp.concatenate(spreads, 1), jnp.concatenate(hots, 1)
        acc_ref[...] += lax.dot_general(spread, hot, (((1,), (1,)), ((), ())), preferred_element_type=F32)

    over_live(n, body)
    both = acc_ref[: 2 * LO, :] + acc_ref[2 * LO :, :]
    for r in range(ROWS):
        part = jnp.concatenate([both[r * LO : (r + 1) * LO], jnp.zeros((LANES - LO, HI), F32)], 0)
        table_ref[pl.ds(r, HI, stride=2), :] = part.T * scale
    lane = lanes8()
    for f in range(FLD):
        for t in range(COLS):
            total = jnp.zeros((8, LANES), F32)
            for q in range(-1, CHUNKS):
                first, last = max(q * CHUNK, t * LANES), min(q * CHUNK + CHUNK, t * LANES + LANES - 1, LON - 1)
                if first > last:
                    continue
                chunk = table_ref[(q % CHUNKS) * 32 + f * 8 : (q % CHUNKS) * 32 + f * 8 + 8, :]
                shift = (q * CHUNK - t * LANES) % LANES
                chunk = pltpu.roll(chunk, shift, 1) if shift else chunk
                mask = (lane >= first - t * LANES) & (lane <= last - t * LANES)
                total += jnp.where(mask, chunk, 0.0)
            adj_ref[t, f * 8 : f * 8 + 8, :] = total
    for t in range(COLS):
        adj = [adj_ref[t, f * 8 : f * 8 + 8, :] for f in range(FLD)]
        for m in range(GROUP):
            total = jnp.zeros((8, LANES), F32)
            for pair in range(FLD // 2):
                ens = ens_ref[m, pair, :, t * LANES : (t + 1) * LANES].astype(F32)
                total += ens[:8] * adj[2 * pair] + ens[8:] * adj[2 * pair + 1]
            proj_ref[t, m * 8 : m * 8 + 8, :] = total

    def store(row, tile):
        out_ref[pl.ds(row, 8, stride=BACK), :] = tile

    pack_rows(lambda m, t: proj_ref[t, m * 8 : m * 8 + 8, :], store, BACK)


def gradient_kernel(alpha_ref, got_ref, out_hbm, out_ref, sems):
    stores = []
    for m in range(GROUP):
        cache = {}
        for t in range(COLS):
            width = min(LANES, LON - t * LANES)
            tile = unpack_tile(got_ref, m, t, cache)
            at = (m, slice(None), slice(None), slice(t * LANES, t * LANES + width))
            out_ref[at] = alpha_ref[at] - tile[:, :width].reshape(LEV, ROWS, width)
        if m % MGRP == MGRP - 1:
            at = slice(m + 1 - MGRP, m + 1)
            stores.append(pltpu.make_async_copy(out_ref.at[at], out_hbm.at[at], sems.at[len(stores)]))
            stores[-1].start()
    for done in stores:
        done.wait()


def shape(*dims, dtype=F32):
    return jax.ShapeDtypeStruct(dims, dtype)


def exchange(x):
    rows = x.shape[0] // TILES
    x = x.reshape(TILES, rows // 2, 2, LANES)
    return lax.all_to_all(x, "tile", 0, 0, tiled=True).reshape(TILES * rows, LANES)


def shards(alpha, ensemble, step_count, obs_index, obs_weight, obs_count, obs_value, inv_var):
    members = GROUP * lax.axis_size("member")
    scale = 1.0 / math.sqrt(members - 1)
    me = lax.axis_index("tile")
    steps = lax.dynamic_slice(step_count, (lax.rem(me, LEV),), (1,))
    counts = obs_count[0]
    member = lax.axis_index("member").reshape(1)
    wide = ((0, 0), (0, COLS * LANES - LON))
    ens = jnp.pad(ensemble.reshape(GROUP, 2, 16, LON), ((0, 0), (0, 0)) + wide)
    value = obs_value.reshape(TILES * OBS_ROWS, LANES)
    var = inv_var.reshape(TILES * OBS_ROWS, LANES)
    flat = shape(TILES * OBS_ROWS, LANES)

    sent = pl.pallas_call(
        pack_kernel,
        out_shape=shape(LAT * THERE, LANES),
        in_specs=[SMEM] + [HBM] * 3,
        out_specs=HBM,
        scratch_shapes=[
            pltpu.VMEM(alpha.shape, F32),
            pltpu.VMEM(value.shape, F32),
            pltpu.VMEM(var.shape, F32),
            pltpu.VMEM((LAT * THERE, LANES), F32),
            pltpu.SemaphoreType.DMA((5,)),
        ],
        compiler_params=params(63),
        name="pack",
    )(member, alpha, value, var)
    got = exchange(sent)

    slots, listed = pl.pallas_call(
        slots_kernel,
        out_shape=(shape(BLOCKS, 8, LANES), shape(LISTED, dtype=I32)),
        in_specs=[SMEM] + [VMEM] * 2,
        out_specs=(VMEM, SMEM),
        compiler_params=params(16),
        cost_estimate=pl.CostEstimate(flops=8000000, bytes_accessed=2097152, transcendentals=0),
        name="slots",
    )(counts, obs_index[0], obs_weight[0])

    buf = [pltpu.VMEM((DEEP, DEEP, 8, LANES), F32)] * 2 + [pltpu.VMEM((DEEP, LANES, LANES), F32)]
    moved, value, var = pl.pallas_call(
        diffuse_first_kernel,
        out_shape=(shape(LAT * BACK, LANES), shape(LAT, LANES), flat),
        in_specs=[SMEM, VMEM],
        out_specs=[VMEM] * 3,
        scratch_shapes=buf,
        compiler_params=params(16),
        name="diffuse_first",
    )(steps, got)
    got = exchange(moved)

    mine = pl.pallas_call(
        lambda *refs: observe_kernel(scale, *refs),
        out_shape=flat,
        in_specs=[SMEM] * 2 + [VMEM] * 4,
        out_specs=VMEM,
        scratch_shapes=[pltpu.VMEM((COLS, 32, LANES), F32), pltpu.VMEM((2 * HI, LANES), F32)],
        compiler_params=params(16),
        name="observe",
    )(member, listed, got, ens, slots, value)
    others = [lax.ppermute(mine, "member", [(i, (i + k) % 4) for i in range(4)]) for k in (1, 3, 2)]

    sent, departure = pl.pallas_call(
        lambda *refs: adjoint_kernel(scale, *refs),
        out_shape=(shape(LAT * BACK, LANES), flat),
        in_specs=[SMEM] * 2 + [VMEM] * 7,
        out_specs=[VMEM] * 2,
        scratch_shapes=[
            pltpu.VMEM((4 * LO, HI), F32),
            pltpu.VMEM((2 * HI, LANES), F32),
            pltpu.VMEM((COLS, 32, LANES), F32),
            pltpu.VMEM((COLS, GROUP * 8, LANES), F32),
        ],
        compiler_params=params(32),
        name="adjoint",
    )(counts, listed, mine, *others, var, slots, ens)
    got = exchange(sent)

    moved = pl.pallas_call(
        diffuse_kernel,
        out_shape=shape(LAT * BACK, LANES),
        in_specs=[SMEM, VMEM],
        out_specs=VMEM,
        scratch_shapes=buf,
        compiler_params=params(16),
        name="diffuse",
    )(steps, got)
    got = exchange(moved)

    gradient = pl.pallas_call(
        gradient_kernel,
        out_shape=shape(*alpha.shape),
        in_specs=[VMEM] * 2,
        out_specs=HBM,
        scratch_shapes=[pltpu.VMEM(alpha.shape, F32), pltpu.SemaphoreType.DMA((PIECES,))],
        compiler_params=params(16),
        name="gradient",
    )(alpha, got)
    return gradient, departure.reshape(1, TILES, SLOT)


def solution(mesh):
    return jax.shard_map(
        shards,
        mesh=mesh,
        in_specs=(
            P("member", None, "tile", None),
            P("member", None, None, "tile", None),
            P(),
            P("tile", None, None, None),
            P("tile", None, None, None),
            P("tile", None),
            P(None, "tile", None),
            P(None, "tile", None),
        ),
        out_specs=(P("member", None, "tile", None), P("tile", None, None)),
        check_vma=False,
    )
```
